128 devices in a mesh: tile: 4 (over x), dev: 32 (over z, y, core).
Axes of the slice: x: 4, y: 4, z: 4, core: 2. Of those that a mesh axis runs over, the one named last changes fastest.
Arguments:
- u_field: float32 [256, 256, 1024], P('dev', 'tile'), may hold values from 0.2 to 1
- v_field: float32 [256, 256, 1024], P('dev', 'tile'), may hold values from 0 to 1
- brick_material: int32 [4, 4, 16], replicated, may hold values from 0 to 3
- color_table: float32 [4, 3, 16], replicated, may hold values from 0 to 2
- alpha_table: float32 [4, 16], replicated, may hold values from 0.002 to 0.02
- assign: int32 [32], replicated, may hold values from 0 to 31, as said below
Outputs:
- u_out: float32 [256, 256, 1024], P('dev', 'tile')
- v_out: float32 [256, 256, 1024], P('dev', 'tile')
- image: float32 [3, 256, 1024], P(None, ('tile', 'dev'))
The draws below stay inside these ranges and needn't reach their ends.
Inputs may be any that keep to these rules, and one draw needn't show every extreme that they name: `assign`: every row block appears once; output blocks g * 8 to g * 8 + 7 take exactly 2 blocks from each brick owner (blocks o * 8 to o * 8 + 7).
All inputs are finite; a program needn't handle non-finite values.
Results may differ from the reference program's by a relative error of at most 0.00039.
Values may be sent and summed in bfloat16 or wider, within the bound.
A program may use at most 384 MiB of HBM per device.

```python
import math
import jax
import jax.numpy as jnp
from jax import lax

NY = 1024
RB = 8
BK = 64
NBIN = 16
NMAT = 4
Z = 256
NX = 256
NB = 8
NBLK = 32
NZB = 4
NXB = 4
NYB = 16


def draw_assign(key, part):
    key = jax.random.fold_in(key, 7)
    groups = NBLK // NB
    share = NB // groups
    first, second = jax.random.split(key)
    owners = jax.vmap(lambda k: jax.random.permutation(k, NB))(jax.random.split(first, groups))
    owners = owners + (jnp.arange(groups, dtype=jnp.int32) * NB)[:, None]
    layout = jnp.transpose(owners.reshape(groups, groups, share), (1, 0, 2)).reshape(groups, NB)
    shuffle = jax.vmap(lambda k: jax.random.permutation(k, NB))(jax.random.split(second, groups))
    result = jnp.take_along_axis(layout, shuffle, axis=1)
    return result.reshape(NBLK).astype(jnp.int32)


def place_ends(array, key, low, top_value):
    longest = array.shape.index(max(array.shape))
    spots = []
    for shift in (0, 1):
        where = [jax.random.randint(jax.random.fold_in(key, axis), (), 0, length) for axis, length in enumerate(array.shape)]
        where[longest] = (where[longest] + shift) % array.shape[longest]
        spots.append(tuple(where))
    return array.at[spots[0]].set(low).at[spots[1]].set(top_value)


def level_of(own_key, extent, cuts, least, high):
    def one(dim, blocks):
        heights = jax.random.uniform(jax.random.fold_in(jax.random.fold_in(own_key, 6), dim), (blocks,), jnp.float32, least / len(cuts), high / len(cuts))
        return jnp.repeat(jnp.exp(heights), extent[dim] // blocks).reshape((-1,) + (1,) * (len(extent) - dim - 1))

    gain = one(*cuts[0])
    for cut in cuts[1:]:
        gain = gain * one(*cut)
    return gain


def setup_inputs(seed: int = 0) -> dict:
    keys = jax.random.split(jax.random.key(seed), 7)
    u_field = jnp.clip(0.2 + 0.8 * jax.random.uniform(keys[0], (Z, NX, NY), jnp.float32) ** level_of(keys[0], (Z, NX, NY), ((0, 32), (1, 4)), -0.2, 0.2), 0.2, 1.0)
    v_field = jnp.clip(1.0 * jax.random.uniform(keys[1], (Z, NX, NY), jnp.float32) ** level_of(keys[1], (Z, NX, NY), ((0, 32), (1, 4)), -0.2, 0.2), 0.0, 1.0)
    brick_material = place_ends(jax.random.randint(keys[2], (NZB, NXB, NYB), 0, NMAT), jax.random.fold_in(keys[2], 1), 0, NMAT - 1).astype(jnp.int32)
    color_table = jnp.clip(jax.random.uniform(keys[3], (NMAT, 3, NBIN), jnp.float32, 0.0, 2.0), 0.0, 2.0)
    alpha_table = jnp.clip(jnp.exp(jax.random.uniform(keys[4], (NMAT, NBIN), jnp.float32, math.log(0.002), math.log(0.02))), 0.002, 0.02)
    assign = draw_assign(jax.random.fold_in(keys[6], 71), 0)
    return {"u_field": u_field, "v_field": v_field, "brick_material": brick_material, "color_table": color_table, "alpha_table": alpha_table, "assign": assign}


def laplace(field):
    centre = field[1:-1, 1:-1]
    sides = jnp.pad(centre, ((0, 0), (0, 0), (1, 1)))
    total = field[2:, 1:-1] + field[:-2, 1:-1] + field[1:-1, 2:] + field[1:-1, :-2]
    total = total + sides[:, :, 2:] + sides[:, :, :-2]
    return total - 6.0 * centre


def react_diffuse(subst, activ):
    s_mid = subst[1:-1, 1:-1]
    a_mid = activ[1:-1, 1:-1]
    feeding = s_mid * a_mid * a_mid
    s_new = s_mid + 0.16 * laplace(subst) - feeding + 0.04 * (1.0 - s_mid)
    a_new = a_mid + 0.08 * laplace(activ) + feeding - 0.1 * a_mid
    return s_new, a_new


def shade(values, material, color_table, alpha_table):
    table = jnp.concatenate([color_table, alpha_table[:, None, :]], axis=1)
    kinds = table.shape[0]
    bins = table.shape[2]
    place = jnp.clip(values, 0.0, 1.0) * (bins - 1)
    result = jnp.zeros((4,) + values.shape, jnp.float32)
    for node in range(bins):
        weight = jnp.maximum(0.0, 1.0 - jnp.abs(place - node))
        chosen = jnp.zeros((4,) + material.shape, jnp.float32)
        for kind in range(kinds):
            chosen = chosen + (material == kind).astype(jnp.float32)[None] * table[kind, :, node].reshape((4,) + (1,) * material.ndim)
        result = result + weight[None] * chosen
    return result


def composite(rgba):
    colour = rgba[:3].astype(jnp.float32)
    alpha = rgba[3].astype(jnp.float32)
    running = jnp.cumprod(1.0 - alpha, axis=0)
    before = jnp.concatenate([jnp.ones_like(running[:1]), running[:-1]], axis=0)
    return jnp.sum(colour * (alpha * before)[None], axis=1)


def reference(u_field, v_field, brick_material, color_table, alpha_table, assign):
    subst, activ = u_field, v_field
    for step in range(2):
        widths = ((1, 1), (1, 1), (0, 0))
        subst, activ = react_diffuse(jnp.pad(subst, widths), jnp.pad(activ, widths))
    z_brick = (jnp.arange(Z, dtype=jnp.int32) // BK).astype(jnp.int32)
    y_brick = (jnp.arange(NY, dtype=jnp.int32) // BK).astype(jnp.int32)

    def render(block):
        start = (block * RB).astype(jnp.int32)
        rows = lax.dynamic_slice_in_dim(activ, start, RB, 1)
        brick_row = (block * RB // BK).astype(jnp.int32)
        bricks = lax.dynamic_index_in_dim(brick_material, brick_row, 1, keepdims=False)
        spread = jnp.take(jnp.take(bricks, z_brick, axis=0), y_brick, axis=1)
        rgba = shade(rows, spread[:, None, :], color_table, alpha_table)
        return composite(rgba.astype(jnp.bfloat16))

    blocks = lax.map(render, assign)
    image = jnp.transpose(blocks, (1, 0, 2, 3)).reshape(3, NX, NY)
    return subst, activ, image
```

```python
import jax
import jax.numpy as jnp
from jax import lax
from jax.experimental import pallas as pl
from jax.experimental.pallas import tpu as pltpu
from jax.sharding import PartitionSpec as P

MESH = pl.DeviceIdType.MESH
I16 = jnp.int16
I32 = jnp.int32
F32 = jnp.float32
DZ, NR, NY = 8, 64, 1024
LT = 8
ROW0 = 8
STEPS, SHIFT = 65534.0, 32767.0
TOPS = (0.32, 0.32, 0.32, 0.16)


def enc(x, top):
    return jnp.round(x * (STEPS / top) - SHIFT).astype(I32).astype(I16)


def dec(x, top):
    return (x.astype(I32).astype(F32) + SHIFT) * (top / STEPS)


def gather(tab, idx):
    return jnp.take_along_axis(tab, idx, axis=1, mode="promise_in_bounds")


def cells(ref, f, j, z0, nz, r0):
    return ref[f, j, pl.ds(z0, nz), pl.ds(r0, 8), :]


def neighbours(ref, f, j, z0, nz, r0, c, lanes):
    depth = cells(ref, f, j, z0 - 1, nz, r0) + cells(ref, f, j, z0 + 1, nz, r0)
    row = cells(ref, f, j, z0, nz, r0 - 1) + cells(ref, f, j, z0, nz, r0 + 1)
    left = pltpu.roll(jnp.where(lanes == 127, cells(ref, f, j - 1, z0, nz, r0), c), 1, 2)
    right = pltpu.roll(jnp.where(lanes == 0, cells(ref, f, j + 1, z0, nz, r0), c), 127, 2)
    return depth + row + (left + right)


def advance(ref, j, z0, nz, r0):
    lanes = lax.broadcasted_iota(I32, (nz, 8, 128), 2)
    u, v = (cells(ref, f, j, z0, nz, r0) for f in range(2))
    su = neighbours(ref, 0, j, z0, nz, r0, u, lanes)
    sv = neighbours(ref, 1, j, z0, nz, r0, v, lanes)
    r = u * v * v
    return 0.16 * su - r + 0.04, 0.08 * sv + (0.42 * v + r)


def kernel(bricks, assign, u, v, color, alpha, u_out, v_out, image, a, b, o, coded, zbuf, tabs, part, slots,
           away, came, pair, got, own, pick, stage, lines, isem, osem, hs, hr, cs, cr, ps, pr, fs, fr, lsem):
    t, d = lax.axis_index("tile"), lax.axis_index("dev")
    nt, nd = lax.axis_size("tile"), lax.axis_size("dev")
    tu, td = lax.rem(t + 1, nt), lax.rem(t + nt - 1, nt)
    du, dd = lax.rem(d + 1, nd), lax.rem(d + nd - 1, nd)
    z, y, core = d // 8, lax.rem(d // 2, 4), lax.rem(d, 2)
    fields, outs = (u, v), (u_out, v_out)
    inz = (d > 0, d < nd - 1)
    inx = (t > 0, t < nt - 1)

    def fetch(f, j):
        return pltpu.make_async_copy(
            fields[f].at[:, :, pl.ds(j * 128, 128)], a.at[f, j + 1, pl.ds(2, DZ), pl.ds(ROW0, NR), :], isem.at[f, j])

    for j in range(LT):
        for f in range(2):
            fetch(f, j).start()

    barrier = pltpu.get_barrier_semaphore()

    def greet(who):
        pl.semaphore_signal(barrier, inc=1, device_id=who, device_id_type=MESH)

    around = [(tt, d2) for tt in (td, t, tu) for d2 in (dd, d, du)]
    around.pop(4)
    for who in around:
        greet(who)

    def chip(k):
        return lax.rem(z + k // 4, 4) * 8 + lax.rem(y + lax.rem(k, 4), 4) * 2 + core

    @pl.loop(1, 16)
    def _(k):
        greet((t, chip(k)))

    rq = lax.rem(d, 4)

    @pl.loop(0, 8)
    def _(k):
        who_t, who_d = lax.rem(t + k // 2, nt), t * 8 + rq * 2 + lax.rem(k, 2)

        @pl.when(jnp.logical_not((who_t == t) & (who_d == d)))
        def _():
            greet((who_t, who_d))

    lanes = lax.broadcasted_iota(I32, (8, 128), 1)
    kf = lax.rem(lanes, 16).astype(F32)
    for j in range(LT):
        for cc in range(4):
            rows = []
            for half in range(2):
                m = bricks[d * DZ // 64, t * NR // 64, 2 * j + half]
                row = color[m, cc] if cc < 3 else alpha[m, 0]
                rows.append(jnp.broadcast_to(row[None], (8, 128)))
            nodes = jnp.where(lanes < 16, rows[0], pltpu.roll(rows[1], 16, 1))
            slope = jnp.where(lax.rem(lanes, 16) == 15, 0.0, pltpu.roll(nodes, 127, 1) - nodes)
            tabs[j, 2 * cc] = nodes - kf * slope
            tabs[j, 2 * cc + 1] = slope

    order = []
    for g in range(4):
        seen = jnp.int32(0)
        found = [jnp.int32(0), jnp.int32(0)]
        for p in range(8):
            w = assign[8 * g + p]
            mine = (w // 8 == t).astype(I32)
            for h in range(2):
                found[h] = found[h] + mine * (seen == h).astype(I32) * lax.rem(w, 8)
            seen = seen + mine
        order += found

    for ref, nz, nr in ((a, DZ + 4, NR + 16), (b, DZ + 2, NR + 8)):
        for f in range(2):
            for j in (0, LT + 1):

                @pl.loop(0, nz)
                def _(k):
                    ref[f, j, k] = jnp.zeros((nr, 128), F32)

    for j in range(LT):
        for f in range(2):
            fetch(f, j).wait()

        @pl.loop(0, 2)
        def _(f):
            for side, z0 in ((0, DZ), (1, 2)):
                for k in range(2):
                    coded[side, j, f, k] = enc(a[f, j + 1, z0 + k, pl.ds(ROW0, NR), :], 1.0)

    pl.semaphore_wait(barrier, 8 + 15 + 8 - ((z == t) & (rq == y)).astype(I32))

    copies = []

    def send(src, dst, who):
        n = len(copies)
        c = pltpu.make_async_remote_copy(src_ref=src, dst_ref=dst, send_sem=hs.at[n], recv_sem=hr.at[n], device_id=who, device_id_type=MESH)
        c.start()
        copies.append(c)

    inner = pl.ds(1, LT)
    for k in range(ZCH):
        js = pl.ds(k * (LT // ZCH), LT // ZCH)
        for side, who in ((0, du), (1, dd)):
            send(coded.at[side, js], zbuf.at[side, js], (t, who))
        if k == 0:
            depth = pl.ds(2, DZ)
            send(a.at[:, inner, depth, pl.ds(ROW0 + NR - 2, 2), :], a.at[:, inner, depth, pl.ds(ROW0 - 2, 2), :], (tu, d))
            send(a.at[:, inner, depth, pl.ds(ROW0, 2), :], a.at[:, inner, depth, pl.ds(ROW0 + NR, 2), :], (td, d))
            for z0, z1, wz in ((DZ + 1, 1, du), (2, DZ + 2, dd)):
                for r0, r1, wx in ((ROW0 + NR - 1, ROW0 - 1, tu), (ROW0, ROW0 + NR, td)):
                    send(a.at[:, inner, z0, pl.ds(r0, 1), :], a.at[:, inner, z1, pl.ds(r1, 1), :], (wx, wz))

    for c in copies[2:8]:
        c.wait()
    for s in range(2):

        @pl.when(jnp.logical_not(inx[s]))
        def _():
            @pl.loop(1, LT + 1)
            def _(j):
                for f in range(2):
                    for k in range(1, DZ + 3):
                        a[f, j, k, pl.ds(ROW0 + NR if s else ROW0 - 2, 2), :] = jnp.zeros((2, 128), F32)

    def first(z0, nz):
        def body(i, carry):
            j, r = 1 + i // 9, lax.rem(i, 9)
            nu, nv = advance(a, j, z0, nz, ROW0 - 1 + 8 * r)
            b[0, j, pl.ds(z0 - 1, nz), pl.ds(8 * r, 8), :] = nu
            b[1, j, pl.ds(z0 - 1, nz), pl.ds(8 * r, 8), :] = nv
            return carry

        lax.fori_loop(0, LT * 9, body, 0, unroll=9)

    def clear_rows(z0, nz):
        for s in range(2):

            @pl.when(jnp.logical_not(inx[s]))
            def _():
                @pl.loop(1, LT + 1)
                def _(j):
                    for f in range(2):
                        for k in range(z0, z0 + nz):
                            b[f, j, k, pl.ds((NR + 1) * s, 1), :] = jnp.zeros((1, 128), F32)

    def second(z0, nz):
        def body(i, carry):
            j, r = i // 8, pl.multiple_of(lax.rem(i, 8) * 8, 8)
            nu, nv = advance(b, j + 1, z0, nz, r + 1)
            o[0, j, pl.ds(z0 - 1, nz), pl.ds(r, 8), :] = nu
            o[1, j, pl.ds(z0 - 1, nz), pl.ds(r, 8), :] = nv
            return carry

        lax.fori_loop(0, LT * 8, body, 0, unroll=8)

    offset = jnp.where(lanes >= 64, 16, 0)

    def shade(j, z0, nz, r):
        keep, total = None, [None] * 3
        for k in range(z0, z0 + nz):
            p = jnp.clip(o[1, j, k, pl.ds(r, 8), :] * 15.0, 0.0, 15.0)
            idx = p.astype(I32) + offset
            vals = []
            for cc in range(4):
                x = gather(tabs[j, 2 * cc], idx) + gather(tabs[j, 2 * cc + 1], idx) * p
                vals.append(x.astype(jnp.bfloat16).astype(F32))
            w = vals[3] if keep is None else vals[3] * keep
            keep = 1.0 - w if keep is None else keep - w
            for cc in range(3):
                x = vals[cc] * w
                total[cc] = x if total[cc] is None else total[cc] + x
        return total, keep

    first(3, 6)
    clear_rows(2, 6)
    second(3, 4)

    def middle(i, carry):
        j, r = i // 8, lax.rem(i, 8)
        total, keep = shade(j, 2, 4, pl.multiple_of(r * 8, 8))
        for cc in range(3):
            part[r, j, cc] = total[cc]
        part[r, j, 3] = keep
        return carry

    lax.fori_loop(0, LT * 8, middle, 0, unroll=4)

    for c in copies[:2] + copies[8:]:
        c.wait()

    @pl.loop(0, LT)
    def _(j):
        for s in range(2):
            for f in range(2):
                for k in range(2):
                    x = dec(zbuf[s, j, f, k], 1.0)
                    a[f, j + 1, (DZ + 2) * s + k, pl.ds(ROW0, NR), :] = jnp.where(inz[s], x, 0.0)

    for s in range(2):

        @pl.when(jnp.logical_not(inz[s]))
        def _():
            @pl.loop(1, LT + 1)
            def _(j):
                for f in range(2):
                    for r in (ROW0 - 1, ROW0 + NR):
                        a[f, j, (DZ + 1) * s + 1, pl.ds(r, 1), :] = jnp.zeros((1, 128), F32)

    first(1, 2)
    first(9, 2)
    clear_rows(0, 2)
    clear_rows(8, 2)
    for s in range(2):

        @pl.when(jnp.logical_not(inz[s]))
        def _():
            @pl.loop(1, LT + 1)
            def _(j):
                for f in range(2):
                    b[f, j, (DZ + 1) * s] = jnp.zeros((NR + 8, 128), F32)

    second(1, 2)
    second(7, 2)

    def emit(f, j):
        return pltpu.make_async_copy(o.at[f, j], outs[f].at[:, :, pl.ds(j * 128, 128)], osem.at[f, j])

    for j in range(LT):
        for f in range(2):
            emit(f, j).start()

    def ends(i, carry):
        j, r = i // 8, lax.rem(i, 8)
        front, keep = shade(j, 0, 2, pl.multiple_of(r * 8, 8))
        back, last = shade(j, 6, 2, pl.multiple_of(r * 8, 8))
        mid = part[r, j, 3]
        for cc in range(3):
            part[r, j, cc] = front[cc] + keep * (part[r, j, cc] + mid * back[cc])
        part[r, j, 3] = 1.0 - keep * mid * last
        return carry

    lax.fori_loop(0, LT * 8, ends, 0, unroll=4)

    for i in range(8):
        for j in range(LT):
            for cc in range(4):
                slots[j // 4, i // 2, cc, pl.ds(2 * (j % 4) + i % 2, 8, stride=8), :] = part[order[i], j, cc]

    def pack(i, carry):
        g, q = i // 4, lax.rem(i, 4)
        for cc in range(4):
            away[g, q, cc] = enc(slots[1 - core, g, cc, pl.ds(pl.multiple_of(16 * q, 16), 16), :], TOPS[cc])
        return carry

    lax.fori_loop(0, 16, pack, 0, unroll=2)
    swap = pltpu.make_async_remote_copy(src_ref=away, dst_ref=came, send_sem=cs, recv_sem=cr, device_id=(t, d + 1 - 2 * core), device_id_type=MESH)
    swap.start()
    swap.wait()

    def join(i, carry):
        g, q = i // 4, lax.rem(i, 4)
        rows = pl.ds(pl.multiple_of(16 * q, 16), 16)
        x = [slots[core, g, cc, rows, :] for cc in range(4)]
        w = [dec(came[g, q, cc], TOPS[cc]) for cc in range(4)]
        ahead = core == 0
        clear = 1.0 - jnp.where(ahead, x[3], w[3])
        for cc in range(4):
            f, s = jnp.where(ahead, x[cc], w[cc]), jnp.where(ahead, w[cc], x[cc])
            pair[g, q, cc] = enc(f + clear * s, 2 * TOPS[cc])
        return carry

    lax.fori_loop(0, 16, join, 0, unroll=2)

    here = z * 4 + y

    def share(k):
        to_z, to_y = lax.rem(z + k // 4, 4), lax.rem(y + lax.rem(k, 4), 4)
        return pltpu.make_async_remote_copy(
            src_ref=pair.at[to_z, to_y], dst_ref=got.at[here], send_sem=ps.at[k], recv_sem=pr.at[k],
            device_id=(t, to_z * 8 + to_y * 2 + core), device_id_type=MESH)

    @pl.loop(1, 16)
    def _(k):
        share(k).start()

    keep_own = pltpu.make_async_copy(pair.at[z, y], got.at[here], lsem)
    keep_own.start()
    keep_own.wait()

    @pl.loop(1, 16)
    def _(k):
        share(k).wait()

    def fold(s, carry):
        keep, total = carry
        x = [dec(got[s, cc], 2 * TOPS[cc]) for cc in range(4)]
        total = tuple(total[cc] + x[cc] * keep for cc in range(3))
        return keep - keep * x[3], total

    zero = jnp.zeros((16, 128), F32)
    _, total = lax.fori_loop(0, 16, fold, (zero + 1.0, (zero, zero, zero)), unroll=4)
    for cc in range(3):
        own[cc] = total[cc]
        for h in range(2):
            pick[h, cc] = own[cc, pl.ds(h, 8, stride=2), :]

    for p in range(8):
        w = assign[8 * z + p] // 8
        s = jnp.int32(0)
        for q in range(p):
            s = s + (assign[8 * z + q] // 8 == w).astype(I32)
        s = jnp.minimum(s, 1)
        for cc in range(3):
            stage[p, cc] = pick[s, cc]

    def spread(k):
        p = lax.rem(k + d // 4, 8)
        return p, (z == t) & (4 * p + y == d), pltpu.make_async_remote_copy(
            src_ref=stage.at[p], dst_ref=lines.at[t, core], send_sem=fs.at[k], recv_sem=fr.at[t, core],
            device_id=(z, 4 * p + y), device_id_type=MESH)

    @pl.loop(0, 8)
    def _(k):
        p, self_, c = spread(k)

        @pl.when(jnp.logical_not(self_))
        def _():
            c.start()

        @pl.when(self_)
        def _():
            pltpu.make_async_copy(stage.at[p], lines.at[t, core], fr.at[t, core]).start()

    @pl.loop(0, 8)
    def _(k):
        p, self_, c = spread(k)

        @pl.when(jnp.logical_not(self_))
        def _():
            c.wait_send()

    for k in range(8):
        pltpu.make_async_copy(stage.at[0], lines.at[k // 2, k % 2], fr.at[k // 2, k % 2]).wait()

    w = assign[8 * t + d // 4] // 8
    for half in range(2):
        for cc in range(3):
            x = lines[w, half, cc]
            for r in range(2):
                for l in range(4):
                    image[cc, r : r + 1, pl.ds((4 * half + l) * 128, 128)] = x[4 * r + l : 4 * r + l + 1]

    for j in range(LT):
        for f in range(2):
            emit(f, j).wait()


ZCH = 4


def local(u, v, bricks, color, alpha, assign):
    hbm = pl.BlockSpec(memory_space=pltpu.HBM)
    smem = pl.BlockSpec(memory_space=pltpu.SMEM)
    vmem = pl.BlockSpec(memory_space=pltpu.VMEM)
    color = jnp.pad(color, ((0, 0), (0, 0), (0, 112)))
    alpha = jnp.pad(alpha[:, None], ((0, 0), (0, 0), (0, 112)))
    dma = pltpu.SemaphoreType.DMA
    return pl.pallas_call(
        kernel,
        out_shape=(
            jax.ShapeDtypeStruct((DZ, NR, NY), F32),
            jax.ShapeDtypeStruct((DZ, NR, NY), F32),
            jax.ShapeDtypeStruct((3, 2, NY), F32),
        ),
        in_specs=[smem, smem, hbm, hbm, vmem, vmem],
        out_specs=(hbm, hbm, vmem),
        scratch_shapes=[
            pltpu.VMEM((2, LT + 2, DZ + 4, NR + 16, 128), F32),
            pltpu.VMEM((2, LT + 2, DZ + 2, NR + 8, 128), F32),
            pltpu.VMEM((2, LT, DZ, NR, 128), F32),
            pltpu.VMEM((2, LT, 2, 2, NR, 128), I16),
            pltpu.VMEM((2, LT, 2, 2, NR, 128), I16),
            pltpu.VMEM((LT, 8, 8, 128), F32),
            pltpu.VMEM((NR // 8, LT, 4, 8, 128), F32),
            pltpu.VMEM((2, 4, 4, NR, 128), F32),
            pltpu.VMEM((4, 4, 4, 16, 128), I16),
            pltpu.VMEM((4, 4, 4, 16, 128), I16),
            pltpu.VMEM((4, 4, 4, 16, 128), I16),
            pltpu.VMEM((16, 4, 16, 128), I16),
            pltpu.VMEM((3, 16, 128), F32),
            pltpu.VMEM((2, 3, 8, 128), F32),
            pltpu.VMEM((8, 3, 8, 128), F32),
            pltpu.VMEM((4, 2, 3, 8, 128), F32),
            dma((2, LT)), dma((2, LT)),
            dma((6 + 2 * ZCH,)), dma((6 + 2 * ZCH,)),
            dma, dma,
            dma((16,)), dma((16,)),
            dma((8,)), dma((4, 2)),
            dma,
        ],
        compiler_params=pltpu.CompilerParams(collective_id=0, has_side_effects=True, vmem_limit_bytes=48 << 20),
        name="reaction_render",
    )(bricks, assign, u, v, color, alpha)


def solution(mesh):
    in_specs = (P("dev", "tile", None), P("dev", "tile", None), P(), P(), P(), P())
    out_specs = (P("dev", "tile", None), P("dev", "tile", None), P(None, ("tile", "dev"), None))
    return jax.shard_map(local, mesh=mesh, in_specs=in_specs, out_specs=out_specs, check_vma=False)
```

```python
import jax
import jax.numpy as jnp
from jax import lax
from jax.experimental import pallas as pl
from jax.experimental.pallas import tpu as pltpu
from jax.sharding import PartitionSpec as P

MESH = pl.DeviceIdType.MESH
I16 = jnp.int16
I32 = jnp.int32
F32 = jnp.float32
DZ, NR, NY = 8, 64, 1024
LT = 8
ROW0 = 8
CU, AU = 2.0**-14, 2.0**-21
STEPS, SHIFT = 65534.0, 32767.0
TOPS = (0.32 / CU, 0.32 / CU, 0.32 / CU, 0.16)
CH = 4


def enc(x, top):
    return jnp.round(x * (STEPS / top) - SHIFT).astype(I32).astype(I16)


def dec(x, top):
    return (x.astype(I32).astype(F32) + SHIFT) * (top / STEPS)


def gather(tab, idx):
    return jnp.take_along_axis(tab, idx, axis=1, mode="promise_in_bounds")


def cells(ref, f, j, z0, nz, r0):
    return ref[f, j, pl.ds(z0, nz), pl.ds(r0, 8), :]


def neighbours(ref, f, j, z0, nz, r0, c, lanes):
    depth = cells(ref, f, j, z0 - 1, nz, r0) + cells(ref, f, j, z0 + 1, nz, r0)
    row = cells(ref, f, j, z0, nz, r0 - 1) + cells(ref, f, j, z0, nz, r0 + 1)
    left = pltpu.roll(jnp.where(lanes == 127, cells(ref, f, j - 1, z0, nz, r0), c), 1, 2)
    right = pltpu.roll(jnp.where(lanes == 0, cells(ref, f, j + 1, z0, nz, r0), c), 127, 2)
    return depth + row + (left + right)


def next_u(ref, j, z0, nz, r0, u, v, lanes):
    return 0.16 * neighbours(ref, 0, j, z0, nz, r0, u, lanes) - u * v * v + 0.04


def next_v(ref, j, z0, nz, r0, u, v, lanes):
    return 0.08 * neighbours(ref, 1, j, z0, nz, r0, v, lanes) + (0.42 * v + u * v * v)


def kernel(bricks_in, assign_in, u, v, color_in, alpha_in, u_out, v_out, image, bricks, assign, color, alpha, nodes, a, b, o,
           coded, zbuf, tabs, part, slots, away, came, pair, got, own, pick, stage, lines, tsem, isem, osem, hs, hr, cs, cr,
           ps, pr, fs, fr, lsem):
    t, d = lax.axis_index("tile"), lax.axis_index("dev")
    nt, nd = lax.axis_size("tile"), lax.axis_size("dev")
    tu, td = lax.rem(t + 1, nt), lax.rem(t + nt - 1, nt)
    du, dd = lax.rem(d + 1, nd), lax.rem(d + nd - 1, nd)
    z, y, core = d // 8, lax.rem(d // 2, 4), lax.rem(d, 2)

    def pair_of(yy):
        return 2 * (1 - lax.rem(yy, 2)) + yy // 2

    def chip_of(q):
        return 2 * lax.rem(q, 2) + 1 - q // 2

    fields, outs = (u, v), (u_out, v_out)
    inz = (d > 0, d < nd - 1)
    inx = (t > 0, t < nt - 1)

    def fetch(f, j):
        return pltpu.make_async_copy(
            fields[f].at[:, :, pl.ds(j * 128, 128)], a.at[f, j + 1, pl.ds(2, DZ), pl.ds(ROW0, NR), :], isem.at[f, j])

    smalls = [pltpu.make_async_copy(x, y_, tsem.at[n]) for n, (x, y_) in enumerate(
        ((bricks_in, bricks), (assign_in, assign), (color_in, color), (alpha_in, alpha)))]
    for c in smalls:
        c.start()
    for j in range(LT):
        for f in range(2):
            fetch(f, j).start()

    barrier = pltpu.get_barrier_semaphore()

    def greet(who):
        pl.semaphore_signal(barrier, inc=1, device_id=who, device_id_type=MESH)

    around = [(tt, d2) for tt in (td, t, tu) for d2 in (dd, d, du)]
    around.pop(4)
    for who in around:
        greet(who)

    def chip(k):
        return lax.rem(z + k // 4, 4) * 8 + lax.rem(y + lax.rem(k, 4), 4) * 2 + core

    @pl.loop(1, 16)
    def _(k):
        greet((t, chip(k)))

    shown = lax.rem(d, 4)

    @pl.loop(0, 8)
    def _(k):
        who_t, who_d = lax.rem(t + k // 2, nt), t * 8 + chip_of(shown) * 2 + lax.rem(k, 2)

        @pl.when(jnp.logical_not((who_t == t) & (who_d == d)))
        def _():
            greet((who_t, who_d))

    for c in smalls:
        c.wait()
    for cc in range(4):
        for m in range(4):
            row = color[cc, m : m + 1, :] if cc < 3 else alpha[m : m + 1, :]
            nodes[m, cc : cc + 1, 0:16] = jnp.round(row * (1 / CU if cc < 3 else 1 / AU)).astype(I32)
    lanes = lax.broadcasted_iota(I32, (8, 128), 1)

    @pl.loop(0, LT)
    def _(j):
        rows = []
        for half in range(2):
            m = bricks[d * DZ // 64, t * NR // 64, 2 * j + half]
            rows.append([jnp.broadcast_to(nodes[m, cc][None], (8, 128)) for cc in range(4)])
        for cc in range(4):
            x = jnp.where(lanes < 16, rows[0][cc], pltpu.roll(rows[1][cc], 16, 1))
            tabs[j, cc] = x * 65536 + pltpu.roll(x, 127, 1)

    order = []
    for g in range(4):
        seen = jnp.int32(0)
        found = [jnp.int32(0), jnp.int32(0)]
        for p in range(8):
            w = assign[8 * g + p]
            mine = (w // 8 == t).astype(I32)
            for h in range(2):
                found[h] = found[h] + mine * (seen == h).astype(I32) * lax.rem(w, 8)
            seen = seen + mine
        order += found

    for ref, nz, nr in ((a, DZ + 4, NR + 16), (b, DZ + 2, NR + 8)):
        for f in range(2):
            for j in (0, LT + 1):

                @pl.loop(0, nz)
                def _(k):
                    ref[f, j, k] = jnp.zeros((nr, 128), F32)

    for j in range(LT):
        for f in range(2):
            fetch(f, j).wait()

        @pl.loop(0, 2)
        def _(f):
            for side, z0 in ((0, DZ), (1, 2)):
                for k in range(2):
                    coded[side, j, f, k] = enc(a[f, j + 1, z0 + k, pl.ds(ROW0, NR), :], 1.0)

    pl.semaphore_wait(barrier, 8 + 15 + 8 - ((z == t) & (shown == pair_of(y))).astype(I32))

    copies = []

    def send(src, dst, who):
        n = len(copies)
        c = pltpu.make_async_remote_copy(src_ref=src, dst_ref=dst, send_sem=hs.at[n], recv_sem=hr.at[n], device_id=who, device_id_type=MESH)
        c.start()
        copies.append(c)

    def tile(e, who):
        return jnp.where(who == 1, e, LT - 1 - e)

    wide = LT // CH
    inner, depth = pl.ds(1, LT), pl.ds(2, DZ)
    for k in range(CH):
        js = pl.ds(jnp.minimum(tile(k * wide, 1 - core), tile(k * wide + wide - 1, 1 - core)), wide)
        for side, who in ((0, du), (1, dd)):
            send(coded.at[side, js], zbuf.at[side, js], (t, who))
        if k == 0:
            send(a.at[:, inner, depth, pl.ds(ROW0 + NR - 2, 2), :], a.at[:, inner, depth, pl.ds(ROW0 - 2, 2), :], (tu, d))
            send(a.at[:, inner, depth, pl.ds(ROW0, 2), :], a.at[:, inner, depth, pl.ds(ROW0 + NR, 2), :], (td, d))
        if k == 1:
            for z0, z1, wz in ((DZ + 1, 1, du), (2, DZ + 2, dd)):
                for r0, r1, wx in ((ROW0 + NR - 1, ROW0 - 1, tu), (ROW0, ROW0 + NR, td)):
                    send(a.at[:, inner, z0, pl.ds(r0, 1), :], a.at[:, inner, z1, pl.ds(r1, 1), :], (wx, wz))
    rows_in, corners_in = copies[2:4], copies[6:10]
    layers_in = [copies[0:2], copies[4:6]] + [copies[10 + 2 * k : 12 + 2 * k] for k in range(CH - 2)]

    def first(j, zs, rs):
        def body(r, carry):
            for z0, nz in zs:
                r0 = ROW0 - 1 + 8 * r
                lane = lax.broadcasted_iota(I32, (nz, 8, 128), 2)
                us, vs = cells(a, 0, j, z0, nz, r0), cells(a, 1, j, z0, nz, r0)
                rows = pl.ds(8 * r, 8)
                b[0, j, pl.ds(z0 - 1, nz), rows, :] = next_u(a, j, z0, nz, r0, us, vs, lane)
                b[1, j, pl.ds(z0 - 1, nz), rows, :] = next_v(a, j, z0, nz, r0, us, vs, lane)
            return carry

        lo, hi, step = rs
        lax.fori_loop(0, (hi - lo) // step + 1, lambda i, c: body(lo + step * i, c), 0, unroll=(hi - lo) // step + 1)
        for s in range(2):

            @pl.when(jnp.logical_not(inx[s]))
            def _():
                for f in range(2):
                    for z0, nz in zs:
                        for k in range(z0 - 1, z0 - 1 + nz):
                            b[f, j, k, pl.ds((NR + 1) * s, 1), :] = jnp.zeros((1, 128), F32)

    def second(f, j, zs):
        def body(r, carry):
            for z0, nz in zs:
                r0 = 8 * r + 1
                lane = lax.broadcasted_iota(I32, (nz, 8, 128), 2)
                us, vs = cells(b, 0, j + 1, z0, nz, r0), cells(b, 1, j + 1, z0, nz, r0)
                o[f, j, pl.ds(z0 - 1, nz), pl.ds(8 * r, 8), :] = (next_v if f else next_u)(b, j + 1, z0, nz, r0, us, vs, lane)
            return carry

        lax.fori_loop(0, 8, body, 0, unroll=8)

    offset = jnp.where(lanes >= 64, 16, 0)

    def shade(j, z0, nz, r):
        keep, total = None, [None] * 3
        for k in range(z0, z0 + nz):
            p = jnp.clip(o[1, j, k, pl.ds(8 * r, 8), :] * 15.0, 0.0, 15.0)
            low = p.astype(I32)
            after = p - low.astype(F32)
            idx, here_ = low + offset, 1.0 - after
            vals = []
            for cc in range(4):
                w = gather(tabs[j, cc], idx)
                x = lax.shift_right_logical(w, 16).astype(F32) * here_ + (w & 65535).astype(F32) * after
                vals.append(x.astype(jnp.bfloat16).astype(F32))
            opacity = vals[3] * AU
            w = opacity if keep is None else opacity * keep
            keep = 1.0 - w if keep is None else keep - w
            for cc in range(3):
                x = vals[cc] * w
                total[cc] = x if total[cc] is None else total[cc] + x
        return total, keep

    def emit(f, j):
        return pltpu.make_async_copy(o.at[f, j], outs[f].at[:, :, pl.ds(j * 128, 128)], osem.at[f, j])

    @pl.loop(1, LT + 1)
    def _(j):
        first(j, ((3, 6),), (1, 7, 1))

    for c in rows_in:
        c.wait_recv()
    for s in range(2):

        @pl.when(jnp.logical_not(inx[s]))
        def _():
            @pl.loop(1, LT + 1)
            def _(j):
                for f in range(2):
                    for k in range(2, DZ + 2):
                        a[f, j, k, pl.ds(ROW0 + NR if s else ROW0 - 2, 2), :] = jnp.zeros((2, 128), F32)

    @pl.loop(1, LT + 1)
    def _(j):
        first(j, ((3, 6),), (0, 8, 8))

    @pl.loop(0, LT)
    def _(j):
        second(1, j, ((3, 4),))

    @pl.loop(0, LT)
    def _(j):
        def middle(r, carry):
            total, keep = shade(j, 2, 4, r)
            for cc in range(3):
                part[r, j, cc] = total[cc]
            part[r, j, 3] = keep
            return carry

        lax.fori_loop(0, 8, middle, 0, unroll=8)

    for c in corners_in:
        c.wait_recv()
    for sz in range(2):
        for sx in range(2):

            @pl.when(jnp.logical_not(inz[sz] & inx[sx]))
            def _():
                @pl.loop(1, LT + 1)
                def _(j):
                    for f in range(2):
                        a[f, j, DZ + 2 if sz else 1, pl.ds(ROW0 + NR if sx else ROW0 - 1, 1), :] = jnp.zeros((1, 128), F32)

    def begin(e):
        j = tile(e, core) + 1
        first(j, ((1, 2), (9, 2)), (0, 8, 1))
        for s in range(2):

            @pl.when(jnp.logical_not(inz[s]))
            def _():
                for f in range(2):
                    b[f, j, (DZ + 1) * s] = jnp.zeros((NR + 8, 128), F32)

    def finish(e):
        j = tile(e, core)
        second(1, j, ((1, 2), (7, 2)))
        emit(1, j).start()

        def ends(r, carry):
            front, keep = shade(j, 0, 2, r)
            back, last = shade(j, 6, 2, r)
            mid = part[r, j, 3]
            for cc in range(3):
                part[r, j, cc] = front[cc] + keep * (part[r, j, cc] + mid * back[cc])
            part[r, j, 3] = 1.0 - keep * mid * last
            return carry

        lax.fori_loop(0, 8, ends, 0, unroll=8)

    def put(half):
        for i in range(8):
            for l in range(4):
                for cc in range(4):
                    slots[half, i // 2, cc, pl.ds(2 * l + i % 2, 8, stride=8), :] = part[order[i], 4 * half + l, cc]

    swap = pltpu.make_async_remote_copy(src_ref=away, dst_ref=came, send_sem=cs, recv_sem=cr, device_id=(t, d + 1 - 2 * core), device_id_type=MESH)

    began = done = 0
    for k in range(CH):
        for c in layers_in[k]:
            c.wait_recv()

        @pl.loop(k * wide, (k + 1) * wide)
        def _(e):
            j = tile(e, core)
            for s in range(2):
                for f in range(2):
                    for i in range(2):
                        x = dec(zbuf[s, j, f, i], 1.0)
                        a[f, j + 1, (DZ + 2) * s + i, pl.ds(ROW0, NR), :] = jnp.where(inz[s], x, 0.0)

        ready = (k + 1) * wide
        last = LT if ready == LT else ready - 1
        pl.loop(began, last)(begin)
        began = last
        last = LT if ready == LT else max(began - 1, 0)
        for lo, hi in ((done, min(last, 4)), (max(done, 4), last)):
            if lo < hi:
                pl.loop(lo, hi)(finish)
                if hi == 4:
                    put(1 - core)

                    def pack(i, carry):
                        g, q = i // 4, lax.rem(i, 4)
                        for cc in range(4):
                            away[g, q, cc] = enc(slots[1 - core, g, cc, pl.ds(pl.multiple_of(16 * q, 16), 16), :], TOPS[cc])
                        return carry

                    lax.fori_loop(0, 16, pack, 0, unroll=4)
                    swap.start()
        done = last
    put(core)
    swap.wait_recv()

    def join(i, carry):
        g, q = i // 4, lax.rem(i, 4)
        rows = pl.ds(pl.multiple_of(16 * q, 16), 16)
        x = [slots[core, g, cc, rows, :] for cc in range(4)]
        w = [dec(came[g, q, cc], TOPS[cc]) for cc in range(4)]
        ahead = core == 0
        clear = 1.0 - jnp.where(ahead, x[3], w[3])
        for cc in range(4):
            f, s = jnp.where(ahead, x[cc], w[cc]), jnp.where(ahead, w[cc], x[cc])
            pair[g, q, cc] = enc(f + clear * s, 2 * TOPS[cc])
        return carry

    lax.fori_loop(0, 16, join, 0, unroll=4)

    here = z * 4 + y

    def share(k, dz, dy):
        to_z, to_y = lax.rem(z + dz, 4), lax.rem(y + dy, 4)
        return pltpu.make_async_remote_copy(
            src_ref=pair.at[to_z, pair_of(to_y)], dst_ref=got.at[here], send_sem=ps.at[k], recv_sem=pr.at[k],
            device_id=(t, to_z * 8 + to_y * 2 + core), device_id_type=MESH)

    far = sorted(((dz, dy) for dz in range(4) for dy in range(4) if dz or dy), key=lambda w: -min(w[0], 4 - w[0]) - min(w[1], 4 - w[1]))
    shares = [share(k, dz, dy) for k, (dz, dy) in enumerate(far)]
    for c in shares:
        c.start()
    keep_own = pltpu.make_async_copy(pair.at[z, pair_of(y)], got.at[here], lsem)
    keep_own.start()

    @pl.loop(0, LT)
    def _(j):
        second(0, j, ((1, 8),))
        emit(0, j).start()

    keep_own.wait()
    for c in shares:
        c.wait_recv()

    def fold(s, carry):
        keep, total = carry
        x = [dec(got[s, cc], 2 * TOPS[cc]) for cc in range(4)]
        total = tuple(total[cc] + x[cc] * keep for cc in range(3))
        return keep - keep * x[3], total

    zero = jnp.zeros((16, 128), F32)
    _, total = lax.fori_loop(0, 16, fold, (zero + 1.0, (zero, zero, zero)), unroll=4)
    for cc in range(3):
        own[cc] = total[cc] * CU
        for h in range(2):
            pick[h, cc] = own[cc, pl.ds(h, 8, stride=2), :]

    for p in range(8):
        w = assign[8 * z + p] // 8
        s = jnp.int32(0)
        for q in range(p):
            s = s + (assign[8 * z + q] // 8 == w).astype(I32)
        s = jnp.minimum(s, 1)
        for cc in range(3):
            stage[p, cc] = pick[s, cc]

    def spread(k):
        p = lax.rem(k + d // 4, 8)
        to = 4 * p + pair_of(y)
        return p, (z == t) & (to == d), pltpu.make_async_remote_copy(
            src_ref=stage.at[p], dst_ref=lines.at[t, core], send_sem=fs.at[k], recv_sem=fr.at[t, core],
            device_id=(z, to), device_id_type=MESH)

    @pl.loop(0, 8)
    def _(k):
        p, self_, c = spread(k)

        @pl.when(jnp.logical_not(self_))
        def _():
            c.start()

        @pl.when(self_)
        def _():
            pltpu.make_async_copy(stage.at[p], lines.at[t, core], fr.at[t, core]).start()

    for k in range(8):
        pltpu.make_async_copy(stage.at[0], lines.at[k // 2, k % 2], fr.at[k // 2, k % 2]).wait()

    w = assign[8 * t + d // 4] // 8
    for half in range(2):
        for cc in range(3):
            x = lines[w, half, cc]
            for r in range(2):
                for l in range(4):
                    image[cc, r : r + 1, pl.ds((4 * half + l) * 128, 128)] = x[4 * r + l : 4 * r + l + 1]

    for c in copies + [swap] + shares:
        c.wait_send()

    @pl.loop(0, 8)
    def _(k):
        p, self_, c = spread(k)

        @pl.when(jnp.logical_not(self_))
        def _():
            c.wait_send()

    for j in range(LT):
        for f in range(2):
            emit(f, j).wait()


def local(u, v, bricks, color, alpha, assign):
    hbm = pl.BlockSpec(memory_space=pltpu.HBM)
    vmem = pl.BlockSpec(memory_space=pltpu.VMEM)
    free = pl.BlockSpec(memory_space=pl.ANY)
    dma = pltpu.SemaphoreType.DMA
    return pl.pallas_call(
        kernel,
        out_shape=(
            jax.ShapeDtypeStruct((DZ, NR, NY), F32),
            jax.ShapeDtypeStruct((DZ, NR, NY), F32),
            jax.ShapeDtypeStruct((3, 2, NY), F32),
        ),
        in_specs=[hbm] * 6,
        out_specs=(free, free, vmem),
        scratch_shapes=[
            pltpu.SMEM((4, 4, 16), I32),
            pltpu.SMEM((32,), I32),
            pltpu.VMEM((3, 4, 16), F32),
            pltpu.VMEM((4, 16), F32),
            pltpu.VMEM((4, 4, 128), I32),
            pltpu.VMEM((2, LT + 2, DZ + 4, NR + 16, 128), F32),
            pltpu.VMEM((2, LT + 2, DZ + 2, NR + 8, 128), F32),
            pltpu.VMEM((2, LT, DZ, NR, 128), F32),
            pltpu.VMEM((2, LT, 2, 2, NR, 128), I16),
            pltpu.VMEM((2, LT, 2, 2, NR, 128), I16),
            pltpu.VMEM((LT, 4, 8, 128), I32),
            pltpu.VMEM((NR // 8, LT, 4, 8, 128), F32),
            pltpu.VMEM((2, 4, 4, NR, 128), F32),
            pltpu.VMEM((4, 4, 4, 16, 128), I16),
            pltpu.VMEM((4, 4, 4, 16, 128), I16),
            pltpu.VMEM((4, 4, 4, 16, 128), I16),
            pltpu.VMEM((16, 4, 16, 128), I16),
            pltpu.VMEM((3, 16, 128), F32),
            pltpu.VMEM((2, 3, 8, 128), F32),
            pltpu.VMEM((8, 3, 8, 128), F32),
            pltpu.VMEM((4, 2, 3, 8, 128), F32),
            dma((4,)), dma((2, LT)), dma((2, LT)),
            dma((6 + 2 * CH,)), dma((6 + 2 * CH,)),
            dma, dma,
            dma((16,)), dma((16,)),
            dma((8,)), dma((4, 2)),
            dma,
        ],
        compiler_params=pltpu.CompilerParams(collective_id=0, has_side_effects=True, vmem_limit_bytes=48 << 20),
        name="reaction_render",
    )(bricks, assign, u, v, jnp.transpose(color, (1, 0, 2)), alpha)


def solution(mesh):
    in_specs = (P("dev", "tile", None), P("dev", "tile", None), P(), P(), P(), P())
    out_specs = (P("dev", "tile", None), P("dev", "tile", None), P(None, ("tile", "dev"), None))
    return jax.shard_map(local, mesh=mesh, in_specs=in_specs, out_specs=out_specs, check_vma=False)
```

```python
import jax
import jax.numpy as jnp
from jax import lax
from jax.experimental import pallas as pl
from jax.experimental.pallas import tpu as pltpu
from jax.sharding import PartitionSpec as P

MESH = pl.DeviceIdType.MESH
I16 = jnp.int16
I32 = jnp.int32
F32 = jnp.float32
DZ, NR, NY = 8, 64, 1024
LT = 8
ROW0 = 8
CU, AU = 2.0**-14, 2.0**-21
STEPS, SHIFT = 65534.0, 32767.0
TOPS = (0.32 / CU, 0.32 / CU, 0.32 / CU, 0.16)
CH = 4


def enc(x, top):
    return jnp.round(x * (STEPS / top) - SHIFT).astype(I32).astype(I16)


def dec(x, top):
    return (x.astype(I32).astype(F32) + SHIFT) * (top / STEPS)


def gather(tab, idx):
    return jnp.take_along_axis(tab, idx, axis=1, mode="promise_in_bounds")


def cells(ref, f, j, z0, nz, r0):
    return ref[f, j, pl.ds(z0, nz), pl.ds(r0, 8), :]


def neighbours(ref, f, j, z0, nz, r0, c, lanes):
    depth = cells(ref, f, j, z0 - 1, nz, r0) + cells(ref, f, j, z0 + 1, nz, r0)
    row = cells(ref, f, j, z0, nz, r0 - 1) + cells(ref, f, j, z0, nz, r0 + 1)
    left = pltpu.roll(jnp.where(lanes == 127, cells(ref, f, j - 1, z0, nz, r0), c), 1, 2)
    right = pltpu.roll(jnp.where(lanes == 0, cells(ref, f, j + 1, z0, nz, r0), c), 127, 2)
    return depth + row + (left + right)


def next_u(ref, j, z0, nz, r0, u, v, lanes):
    return 0.16 * neighbours(ref, 0, j, z0, nz, r0, u, lanes) - u * v * v + 0.04


def next_v(ref, j, z0, nz, r0, u, v, lanes):
    return 0.08 * neighbours(ref, 1, j, z0, nz, r0, v, lanes) + (0.42 * v + u * v * v)


def kernel(bricks_in, assign_in, u, v, color_in, alpha_in, u_out, v_out, image, bricks, assign, color, alpha, nodes, a, b, o,
           coded, zbuf, tabs, part, slots, away, came, pair, got, own, pick, stage, lines, tsem, isem, osem, hs, hr, cs, cr,
           ps, pr, fs, fr, lsem):
    t, d = lax.axis_index("tile"), lax.axis_index("dev")
    nt, nd = lax.axis_size("tile"), lax.axis_size("dev")
    tu, td = lax.rem(t + 1, nt), lax.rem(t + nt - 1, nt)
    du, dd = lax.rem(d + 1, nd), lax.rem(d + nd - 1, nd)
    z, y, core = d // 8, lax.rem(d // 2, 4), lax.rem(d, 2)

    def pair_of(yy):
        return 2 * (1 - lax.rem(yy, 2)) + yy // 2

    def chip_of(q):
        return 2 * lax.rem(q, 2) + 1 - q // 2

    fields, outs = (u, v), (u_out, v_out)
    inz = (d > 0, d < nd - 1)
    inx = (t > 0, t < nt - 1)

    def fetch(f, j):
        return pltpu.make_async_copy(
            fields[f].at[:, :, pl.ds(j * 128, 128)], a.at[f, j + 1, pl.ds(2, DZ), pl.ds(ROW0, NR), :], isem.at[f, j])

    smalls = [pltpu.make_async_copy(x, y_, tsem.at[n]) for n, (x, y_) in enumerate(
        ((bricks_in, bricks), (assign_in, assign), (color_in, color), (alpha_in, alpha)))]
    for c in smalls:
        c.start()
    for j in range(LT):
        for f in range(2):
            fetch(f, j).start()

    barrier = pltpu.get_barrier_semaphore()

    def greet(who):
        pl.semaphore_signal(barrier, inc=1, device_id=who, device_id_type=MESH)

    around = [(tt, d2) for tt in (td, t, tu) for d2 in (dd, d, du)]
    around.pop(4)
    for who in around:
        greet(who)

    def chip(k):
        return lax.rem(z + k // 4, 4) * 8 + lax.rem(y + lax.rem(k, 4), 4) * 2 + core

    @pl.loop(1, 16)
    def _(k):
        greet((t, chip(k)))

    shown = lax.rem(d, 4)

    @pl.loop(0, 8)
    def _(k):
        who_t, who_d = lax.rem(t + k // 2, nt), t * 8 + chip_of(shown) * 2 + lax.rem(k, 2)

        @pl.when(jnp.logical_not((who_t == t) & (who_d == d)))
        def _():
            greet((who_t, who_d))

    for c in smalls:
        c.wait()
    for cc in range(4):
        for m in range(4):
            row = color[cc, m : m + 1, :] if cc < 3 else alpha[m : m + 1, :]
            nodes[m, cc : cc + 1, 0:16] = jnp.round(row * (1 / CU if cc < 3 else 1 / AU)).astype(I32)
    lanes = lax.broadcasted_iota(I32, (8, 128), 1)

    @pl.loop(0, LT)
    def _(j):
        rows = []
        for half in range(2):
            m = bricks[d * DZ // 64, t * NR // 64, 2 * j + half]
            rows.append([jnp.broadcast_to(nodes[m, cc][None], (8, 128)) for cc in range(4)])
        for cc in range(4):
            x = jnp.where(lanes < 16, rows[0][cc], pltpu.roll(rows[1][cc], 16, 1))
            tabs[j, cc] = x * 65536 + pltpu.roll(x, 127, 1)

    order = []
    for g in range(4):
        seen = jnp.int32(0)
        found = [jnp.int32(0), jnp.int32(0)]
        for p in range(8):
            w = assign[8 * g + p]
            mine = (w // 8 == t).astype(I32)
            for h in range(2):
                found[h] = found[h] + mine * (seen == h).astype(I32) * lax.rem(w, 8)
            seen = seen + mine
        order += found

    for ref, nz, nr in ((a, DZ + 4, NR + 16), (b, DZ + 2, NR + 8)):
        for f in range(2):
            for j in (0, LT + 1):

                @pl.loop(0, nz)
                def _(k):
                    ref[f, j, k] = jnp.zeros((nr, 128), F32)

    for j in range(LT):
        for f in range(2):
            fetch(f, j).wait()

        @pl.loop(0, 2)
        def _(f):
            for side, z0 in ((0, DZ), (1, 2)):
                for k in range(2):
                    coded[side, j, f, k] = enc(a[f, j + 1, z0 + k, pl.ds(ROW0, NR), :], 1.0)

    pl.semaphore_wait(barrier, 8 + 15 + 8 - ((z == t) & (shown == pair_of(y))).astype(I32))

    copies = []

    def send(src, dst, who):
        n = len(copies)
        c = pltpu.make_async_remote_copy(src_ref=src, dst_ref=dst, send_sem=hs.at[n], recv_sem=hr.at[n], device_id=who, device_id_type=MESH)
        c.start()
        copies.append(c)

    def tile(e, who):
        return jnp.where(who == 1, e, LT - 1 - e)

    wide = LT // CH
    inner, depth = pl.ds(1, LT), pl.ds(2, DZ)
    for k in range(CH):
        js = pl.ds(jnp.minimum(tile(k * wide, 1 - core), tile(k * wide + wide - 1, 1 - core)), wide)
        for side, who in ((0, du), (1, dd)):
            send(coded.at[side, js], zbuf.at[side, js], (t, who))
        if k == 0:
            send(a.at[:, inner, depth, pl.ds(ROW0 + NR - 2, 2), :], a.at[:, inner, depth, pl.ds(ROW0 - 2, 2), :], (tu, d))
            send(a.at[:, inner, depth, pl.ds(ROW0, 2), :], a.at[:, inner, depth, pl.ds(ROW0 + NR, 2), :], (td, d))
        if k == 1:
            for z0, z1, wz in ((DZ + 1, 1, du), (2, DZ + 2, dd)):
                for r0, r1, wx in ((ROW0 + NR - 1, ROW0 - 1, tu), (ROW0, ROW0 + NR, td)):
                    send(a.at[:, inner, z0, pl.ds(r0, 1), :], a.at[:, inner, z1, pl.ds(r1, 1), :], (wx, wz))
    rows_in, corners_in = copies[2:4], copies[6:10]
    layers_in = [copies[0:2], copies[4:6]] + [copies[10 + 2 * k : 12 + 2 * k] for k in range(CH - 2)]

    def steps(body, rs):
        lo, hi, step = rs
        n = (hi - lo) // step + 1
        lax.fori_loop(0, n, lambda i, c: body(lo + step * i, c), 0, unroll=n)

    def first(j, zs, rs):
        def body(r, carry):
            for z0, nz in zs:
                r0 = ROW0 - 1 + 8 * r
                lane = lax.broadcasted_iota(I32, (nz, 8, 128), 2)
                us, vs = cells(a, 0, j, z0, nz, r0), cells(a, 1, j, z0, nz, r0)
                rows = pl.ds(8 * r, 8)
                b[0, j, pl.ds(z0 - 1, nz), rows, :] = next_u(a, j, z0, nz, r0, us, vs, lane)
                b[1, j, pl.ds(z0 - 1, nz), rows, :] = next_v(a, j, z0, nz, r0, us, vs, lane)
            return carry

        steps(body, rs)
        for s in range(2):

            @pl.when(jnp.logical_not(inx[s]))
            def _():
                for f in range(2):
                    for z0, nz in zs:
                        for k in range(z0 - 1, z0 - 1 + nz):
                            b[f, j, k, pl.ds((NR + 1) * s, 1), :] = jnp.zeros((1, 128), F32)

    def second(f, j, zs, rs=(0, 7, 1)):
        def body(r, carry):
            for z0, nz in zs:
                r0 = 8 * r + 1
                lane = lax.broadcasted_iota(I32, (nz, 8, 128), 2)
                us, vs = cells(b, 0, j + 1, z0, nz, r0), cells(b, 1, j + 1, z0, nz, r0)
                o[f, j, pl.ds(z0 - 1, nz), pl.ds(8 * r, 8), :] = (next_v if f else next_u)(b, j + 1, z0, nz, r0, us, vs, lane)
            return carry

        steps(body, rs)

    offset = jnp.where(lanes >= 64, 16, 0)

    def shade(j, z0, nz, r):
        keep, total = None, [None] * 3
        for k in range(z0, z0 + nz):
            p = jnp.clip(o[1, j, k, pl.ds(8 * r, 8), :] * 15.0, 0.0, 15.0)
            low = p.astype(I32)
            after = p - low.astype(F32)
            idx, here_ = low + offset, 1.0 - after
            vals = []
            for cc in range(4):
                w = gather(tabs[j, cc], idx)
                x = lax.shift_right_logical(w, 16).astype(F32) * here_ + (w & 65535).astype(F32) * after
                vals.append(x.astype(jnp.bfloat16).astype(F32))
            opacity = vals[3] * AU
            w = opacity if keep is None else opacity * keep
            keep = 1.0 - w if keep is None else keep - w
            for cc in range(3):
                x = vals[cc] * w
                total[cc] = x if total[cc] is None else total[cc] + x
        return total, keep

    def emit(f, j):
        return pltpu.make_async_copy(o.at[f, j], outs[f].at[:, :, pl.ds(j * 128, 128)], osem.at[f, j])

    def middle(j, rs):
        def body(r, carry):
            total, keep = shade(j, 2, 4, r)
            for cc in range(3):
                part[r, j, cc] = total[cc]
            part[r, j, 3] = keep
            return carry

        steps(body, rs)

    @pl.loop(1, LT + 1)
    def _(j):
        first(j, ((3, 6),), (1, 7, 1))

    @pl.loop(0, LT)
    def _(j):
        second(1, j, ((3, 4),), (1, 6, 1))

    @pl.loop(0, LT)
    def _(j):
        middle(j, (1, 6, 1))

    for c in rows_in:
        c.wait_recv()
    for s in range(2):

        @pl.when(jnp.logical_not(inx[s]))
        def _():
            @pl.loop(1, LT + 1)
            def _(j):
                for f in range(2):
                    for k in range(2, DZ + 2):
                        a[f, j, k, pl.ds(ROW0 + NR if s else ROW0 - 2, 2), :] = jnp.zeros((2, 128), F32)

    @pl.loop(1, LT + 1, unroll=2)
    def _(j):
        first(j, ((3, 6),), (0, 8, 8))

    @pl.loop(0, LT, unroll=4)
    def _(j):
        second(1, j, ((3, 4),), (0, 7, 7))

    @pl.loop(0, LT, unroll=4)
    def _(j):
        middle(j, (0, 7, 7))

    for c in corners_in:
        c.wait_recv()
    for sz in range(2):
        for sx in range(2):

            @pl.when(jnp.logical_not(inz[sz] & inx[sx]))
            def _():
                @pl.loop(1, LT + 1)
                def _(j):
                    for f in range(2):
                        a[f, j, DZ + 2 if sz else 1, pl.ds(ROW0 + NR if sx else ROW0 - 1, 1), :] = jnp.zeros((1, 128), F32)

    def begin(e):
        j = tile(e, core) + 1
        first(j, ((1, 2), (9, 2)), (0, 8, 1))
        for s in range(2):

            @pl.when(jnp.logical_not(inz[s]))
            def _():
                for f in range(2):
                    b[f, j, (DZ + 1) * s] = jnp.zeros((NR + 8, 128), F32)

    def finish(e):
        j = tile(e, core)
        second(1, j, ((1, 2), (7, 2)))
        emit(1, j).start()

        def ends(r, carry):
            front, keep = shade(j, 0, 2, r)
            back, last = shade(j, 6, 2, r)
            mid = part[r, j, 3]
            for cc in range(3):
                part[r, j, cc] = front[cc] + keep * (part[r, j, cc] + mid * back[cc])
            part[r, j, 3] = 1.0 - keep * mid * last
            return carry

        lax.fori_loop(0, 8, ends, 0, unroll=8)

    def put(half):
        for i in range(8):
            for l in range(4):
                for cc in range(4):
                    slots[half, i // 2, cc, pl.ds(2 * l + i % 2, 8, stride=8), :] = part[order[i], 4 * half + l, cc]

    swap = pltpu.make_async_remote_copy(src_ref=away, dst_ref=came, send_sem=cs, recv_sem=cr, device_id=(t, d + 1 - 2 * core), device_id_type=MESH)

    began = done = 0
    for k in range(CH):
        for c in layers_in[k]:
            c.wait_recv()

        @pl.loop(k * wide, (k + 1) * wide)
        def _(e):
            j = tile(e, core)
            for s in range(2):
                for f in range(2):
                    for i in range(2):
                        x = dec(zbuf[s, j, f, i], 1.0)
                        a[f, j + 1, (DZ + 2) * s + i, pl.ds(ROW0, NR), :] = jnp.where(inz[s], x, 0.0)

        ready = (k + 1) * wide
        last = LT if ready == LT else ready - 1
        pl.loop(began, last)(begin)
        began = last
        last = LT if ready == LT else max(began - 1, 0)
        for lo, hi in ((done, min(last, 4)), (max(done, 4), last)):
            if lo < hi:
                pl.loop(lo, hi)(finish)
                if hi == 4:
                    put(1 - core)

                    def pack(i, carry):
                        g, q = i // 4, lax.rem(i, 4)
                        for cc in range(4):
                            away[g, q, cc] = enc(slots[1 - core, g, cc, pl.ds(pl.multiple_of(16 * q, 16), 16), :], TOPS[cc])
                        return carry

                    lax.fori_loop(0, 16, pack, 0, unroll=4)
                    swap.start()
        done = last
    put(core)
    swap.wait_recv()

    def join(i, carry):
        g, q = i // 4, lax.rem(i, 4)
        rows = pl.ds(pl.multiple_of(16 * q, 16), 16)
        x = [slots[core, g, cc, rows, :] for cc in range(4)]
        w = [dec(came[g, q, cc], TOPS[cc]) for cc in range(4)]
        ahead = core == 0
        clear = 1.0 - jnp.where(ahead, x[3], w[3])
        for cc in range(4):
            f, s = jnp.where(ahead, x[cc], w[cc]), jnp.where(ahead, w[cc], x[cc])
            pair[g, q, cc] = enc(f + clear * s, 2 * TOPS[cc])
        return carry

    lax.fori_loop(0, 16, join, 0, unroll=4)

    here = z * 4 + y
    owners = [assign[8 * z + p] // 8 for p in range(8)]
    which = []
    for p in range(8):
        n = jnp.int32(0)
        for q in range(p):
            n = n + (owners[q] == owners[p]).astype(I32)
        which.append(jnp.minimum(n, 1))

    def share(k, dz, dy):
        to_z, to_y = lax.rem(z + dz, 4), lax.rem(y + dy, 4)
        return pltpu.make_async_remote_copy(
            src_ref=pair.at[to_z, pair_of(to_y)], dst_ref=got.at[here], send_sem=ps.at[k], recv_sem=pr.at[k],
            device_id=(t, to_z * 8 + to_y * 2 + core), device_id_type=MESH)

    far = sorted(((dz, dy) for dz in range(4) for dy in range(4) if dz or dy), key=lambda w: -min(w[0], 4 - w[0]) - min(w[1], 4 - w[1]))
    shares = [share(k, dz, dy) for k, (dz, dy) in enumerate(far)]
    for c in shares:
        c.start()
    keep_own = pltpu.make_async_copy(pair.at[z, pair_of(y)], got.at[here], lsem)
    keep_own.start()

    @pl.loop(0, LT)
    def _(j):
        second(0, j, ((1, 8),))
        emit(0, j).start()

    keep_own.wait()
    for c in shares:
        c.wait_recv()

    def fold(s, carry):
        keep, total = carry
        x = [dec(got[s, cc], 2 * TOPS[cc]) for cc in range(4)]
        total = tuple(total[cc] + x[cc] * keep for cc in range(3))
        return keep - keep * x[3], total

    zero = jnp.zeros((16, 128), F32)
    _, total = lax.fori_loop(0, 16, fold, (zero + 1.0, (zero, zero, zero)), unroll=4)
    for cc in range(3):
        own[cc] = total[cc] * CU
        for h in range(2):
            pick[h, cc] = own[cc, pl.ds(h, 8, stride=2), :]

    for p in range(8):
        for cc in range(3):
            stage[p, cc] = pick[which[p], cc]

    def spread(k):
        p = lax.rem(k + d // 4, 8)
        to = 4 * p + pair_of(y)
        return p, (z == t) & (to == d), pltpu.make_async_remote_copy(
            src_ref=stage.at[p], dst_ref=lines.at[t, core], send_sem=fs.at[k], recv_sem=fr.at[t, core],
            device_id=(z, to), device_id_type=MESH)

    @pl.loop(0, 8)
    def _(k):
        p, self_, c = spread(k)

        @pl.when(jnp.logical_not(self_))
        def _():
            c.start()

        @pl.when(self_)
        def _():
            pltpu.make_async_copy(stage.at[p], lines.at[t, core], fr.at[t, core]).start()

    for k in range(8):
        pltpu.make_async_copy(stage.at[0], lines.at[k // 2, k % 2], fr.at[k // 2, k % 2]).wait()

    w = assign[8 * t + d // 4] // 8
    for half in range(2):
        for cc in range(3):
            x = lines[w, half, cc]
            for r in range(2):
                for l in range(4):
                    image[cc, r : r + 1, pl.ds((4 * half + l) * 128, 128)] = x[4 * r + l : 4 * r + l + 1]

    for c in copies + [swap] + shares:
        c.wait_send()

    @pl.loop(0, 8)
    def _(k):
        p, self_, c = spread(k)

        @pl.when(jnp.logical_not(self_))
        def _():
            c.wait_send()

    for j in range(LT):
        for f in range(2):
            emit(f, j).wait()


def write(u, v, image, u_out, v_out, image_out, sem, isem):
    copies = [pltpu.make_async_copy(image, image_out, isem)]
    for f, (x, y) in enumerate(((u, u_out), (v, v_out))):
        copies += [pltpu.make_async_copy(x.at[k], y.at[k], sem.at[f, k]) for k in range(DZ)]
    for c in copies:
        c.start()
    for c in copies:
        c.wait()


def local(u, v, bricks, color, alpha, assign):
    hbm = pl.BlockSpec(memory_space=pltpu.HBM)
    vmem = pl.BlockSpec(memory_space=pltpu.VMEM)
    free = pl.BlockSpec(memory_space=pl.ANY)
    dma = pltpu.SemaphoreType.DMA
    u, v, image = pl.pallas_call(
        kernel,
        out_shape=(
            jax.ShapeDtypeStruct((DZ, NR, NY), F32),
            jax.ShapeDtypeStruct((DZ, NR, NY), F32),
            jax.ShapeDtypeStruct((3, 2, NY), F32),
        ),
        in_specs=[hbm] * 6,
        out_specs=(free, free, vmem),
        scratch_shapes=[
            pltpu.SMEM((4, 4, 16), I32),
            pltpu.SMEM((32,), I32),
            pltpu.VMEM((3, 4, 16), F32),
            pltpu.VMEM((4, 16), F32),
            pltpu.VMEM((4, 4, 128), I32),
            pltpu.VMEM((2, LT + 2, DZ + 4, NR + 16, 128), F32),
            pltpu.VMEM((2, LT + 2, DZ + 2, NR + 8, 128), F32),
            pltpu.VMEM((2, LT, DZ, NR, 128), F32),
            pltpu.VMEM((2, LT, 2, 2, NR, 128), I16),
            pltpu.VMEM((2, LT, 2, 2, NR, 128), I16),
            pltpu.VMEM((LT, 4, 8, 128), I32),
            pltpu.VMEM((NR // 8, LT, 4, 8, 128), F32),
            pltpu.VMEM((2, 4, 4, NR, 128), F32),
            pltpu.VMEM((4, 4, 4, 16, 128), I16),
            pltpu.VMEM((4, 4, 4, 16, 128), I16),
            pltpu.VMEM((4, 4, 4, 16, 128), I16),
            pltpu.VMEM((16, 4, 16, 128), I16),
            pltpu.VMEM((3, 16, 128), F32),
            pltpu.VMEM((2, 3, 8, 128), F32),
            pltpu.VMEM((8, 3, 8, 128), F32),
            pltpu.VMEM((4, 2, 3, 8, 128), F32),
            dma((4,)), dma((2, LT)), dma((2, LT)),
            dma((6 + 2 * CH,)), dma((6 + 2 * CH,)),
            dma, dma,
            dma((16,)), dma((16,)),
            dma((8,)), dma((4, 2)),
            dma,
        ],
        compiler_params=pltpu.CompilerParams(collective_id=0, has_side_effects=True, vmem_limit_bytes=48 << 20),
        name="reaction_render",
    )(*[pltpu.with_memory_space_constraint(x, pltpu.HBM) for x in (bricks, assign, u, v, jnp.transpose(color, (1, 0, 2)), alpha)])
    return pl.pallas_call(
        write,
        out_shape=(
            jax.ShapeDtypeStruct((DZ, NR, NY), F32),
            jax.ShapeDtypeStruct((DZ, NR, NY), F32),
            jax.ShapeDtypeStruct((3, 2, NY), F32),
        ),
        in_specs=[free] * 3,
        out_specs=(hbm, hbm, hbm),
        scratch_shapes=[dma((2, DZ)), dma],
        compiler_params=pltpu.CompilerParams(vmem_limit_bytes=1 << 20),
        name="write",
    )(u, v, image)


def solution(mesh):
    in_specs = (P("dev", "tile", None), P("dev", "tile", None), P(), P(), P(), P())
    out_specs = (P("dev", "tile", None), P("dev", "tile", None), P(None, ("tile", "dev"), None))
    return jax.shard_map(local, mesh=mesh, in_specs=in_specs, out_specs=out_specs, check_vma=False)
```

```python
import jax
import jax.numpy as jnp
from jax import lax
from jax.experimental import pallas as pl
from jax.experimental.pallas import tpu as pltpu
from jax.sharding import PartitionSpec as P

MESH = pl.DeviceIdType.MESH
I16 = jnp.int16
I32 = jnp.int32
F32 = jnp.float32
DZ, NR, NY = 8, 64, 1024
LT = 8
ROW0 = 8
CU, AU = 2.0**-14, 2.0**-21
STEPS, SHIFT = 65534.0, 32767.0
TOPS = (0.32 / CU, 0.32 / CU, 0.32 / CU, 0.16)
TOP = 2.01 / CU
CH = 4


def enc(x, top):
    return jnp.round(x * (STEPS / top) - SHIFT).astype(I32).astype(I16)


def dec(x, top):
    return (x.astype(I32).astype(F32) + SHIFT) * (top / STEPS)


def gather(tab, idx):
    return jnp.take_along_axis(tab, idx, axis=1, mode="promise_in_bounds")


def cells(ref, f, j, z0, nz, r0):
    return ref[f, j, pl.ds(z0, nz), pl.ds(r0, 8), :]


def neighbours(ref, f, j, z0, nz, r0, c, lanes):
    depth = cells(ref, f, j, z0 - 1, nz, r0) + cells(ref, f, j, z0 + 1, nz, r0)
    row = cells(ref, f, j, z0, nz, r0 - 1) + cells(ref, f, j, z0, nz, r0 + 1)
    left = pltpu.roll(jnp.where(lanes == 127, cells(ref, f, j - 1, z0, nz, r0), c), 1, 2)
    right = pltpu.roll(jnp.where(lanes == 0, cells(ref, f, j + 1, z0, nz, r0), c), 127, 2)
    return depth + row + (left + right)


def next_u(ref, j, z0, nz, r0, u, v, lanes):
    return 0.16 * neighbours(ref, 0, j, z0, nz, r0, u, lanes) - u * v * v + 0.04


def next_v(ref, j, z0, nz, r0, u, v, lanes):
    return 0.08 * neighbours(ref, 1, j, z0, nz, r0, v, lanes) + (0.42 * v + u * v * v)


def kernel(bricks_in, assign_in, u, v, color_in, alpha_in, u_out, v_out, image, bricks, assign, color, alpha, nodes, unit, a, b, o,
           coded, zbuf, tabs, part, slots, away, came, pair, got, own, pick, stage, lines, told, tsem, isem, osem, hs, hr, cs, cr,
           ps, pr, fs, fr, lsem):
    t, d = lax.axis_index("tile"), lax.axis_index("dev")
    nt, nd = lax.axis_size("tile"), lax.axis_size("dev")
    tu, td = lax.rem(t + 1, nt), lax.rem(t + nt - 1, nt)
    du, dd = lax.rem(d + 1, nd), lax.rem(d + nd - 1, nd)
    z, y, core = d // 8, lax.rem(d // 2, 4), lax.rem(d, 2)

    def pair_of(yy):
        return 2 * (1 - lax.rem(yy, 2)) + yy // 2

    def chip_of(q):
        return 2 * lax.rem(q, 2) + 1 - q // 2

    fields, outs = (u, v), (u_out, v_out)
    inz = (d > 0, d < nd - 1)
    inx = (t > 0, t < nt - 1)

    def fetch(f, j):
        return pltpu.make_async_copy(
            fields[f].at[:, :, pl.ds(j * 128, 128)], a.at[f, j + 1, pl.ds(2, DZ), pl.ds(ROW0, NR), :], isem.at[f, j])

    smalls = [pltpu.make_async_copy(x, y_, tsem.at[n]) for n, (x, y_) in enumerate(
        ((bricks_in, bricks), (assign_in, assign), (color_in, color), (alpha_in, alpha)))]
    for c in smalls:
        c.start()
    def tile(e, who):
        return jnp.where(who == 1, e, LT - 1 - e)

    for e in range(LT):
        for f in range(2):
            fetch(f, tile(e, 1 - core)).start()

    barrier = pltpu.get_barrier_semaphore()

    def greet(who):
        pl.semaphore_signal(barrier, inc=1, device_id=who, device_id_type=MESH)

    around = [(tt, d2) for tt in (td, t, tu) for d2 in (dd, d, du)]
    around.pop(4)
    def chip(zz, yy):
        return (t, lax.rem(zz, 4) * 8 + lax.rem(yy, 4) * 2 + core)

    sides_y = (chip(z, y + 1), chip(z, y + 3))
    sides_z = (chip(z + 1, y), chip(z + 3, y))
    sides_x = ((tu, d), (td, d))
    around += sides_y + sides_z
    for who in around:
        greet(who)

    shown = lax.rem(d, 4)

    rounds = (sides_y, sides_z, sides_z, sides_x, sides_x, ((t, d + 1 - 2 * core),))

    def tell(n):
        for who in rounds[n]:
            pl.semaphore_signal(told.at[n], inc=1, device_id=who, device_id_type=MESH)

    def hear(n):
        pl.semaphore_wait(told.at[n], len(rounds[n]))
        if n + 1 < len(rounds):
            tell(n + 1)

    for c in smalls:
        c.wait()
    largest = color[0]
    for cc in (1, 2):
        largest = jnp.maximum(largest, color[cc])
    largest = jnp.max(jnp.max(largest, axis=0, keepdims=True), axis=1, keepdims=True)
    up = jnp.ones((1, 1), F32)
    for n in (8, 4, 2, 1):
        up = jnp.where(largest * up * 2.0**n <= 2.0, up * 2.0**n, up)
    unit[...] = jnp.broadcast_to(up, (8, 128))
    for cc in range(4):
        for m in range(4):
            row = color[cc, m : m + 1, :] if cc < 3 else alpha[m : m + 1, :]
            nodes[m, cc : cc + 1, 0:16] = jnp.round(row * up * (1 / CU) if cc < 3 else row * (1 / AU)).astype(I32)
    lanes = lax.broadcasted_iota(I32, (8, 128), 1)

    @pl.loop(0, LT)
    def _(j):
        rows = []
        for half in range(2):
            m = bricks[d * DZ // 64, t * NR // 64, 2 * j + half]
            rows.append([jnp.broadcast_to(nodes[m, cc][None], (8, 128)) for cc in range(4)])
        for cc in range(4):
            x = jnp.where(lanes < 16, rows[0][cc], pltpu.roll(rows[1][cc], 16, 1))
            tabs[j, cc] = x * 65536 + pltpu.roll(x, 127, 1)

    order = []
    for g in range(4):
        seen = jnp.int32(0)
        found = [jnp.int32(0), jnp.int32(0)]
        for p in range(8):
            w = assign[8 * g + p]
            mine = (w // 8 == t).astype(I32)
            for h in range(2):
                found[h] = found[h] + mine * (seen == h).astype(I32) * lax.rem(w, 8)
            seen = seen + mine
        order += found

    for ref, nz, nr in ((a, DZ + 4, NR + 16), (b, DZ + 2, NR + 8)):
        for f in range(2):
            for j in (0, LT + 1):

                @pl.loop(0, nz)
                def _(k):
                    ref[f, j, k] = jnp.zeros((nr, 128), F32)

    copies = []

    def send(src, dst, who):
        n = len(copies)
        c = pltpu.make_async_remote_copy(src_ref=src, dst_ref=dst, send_sem=hs.at[n], recv_sem=hr.at[n], device_id=who, device_id_type=MESH)
        c.start()
        copies.append(c)

    wide = LT // CH
    inner, depth = pl.ds(1, LT), pl.ds(2, DZ)
    for k in range(CH):

        @pl.loop(k * wide, (k + 1) * wide)
        def _(e):
            j = tile(e, 1 - core)
            for f in range(2):
                fetch(f, j).wait()
                for side, z0 in ((0, DZ), (1, 2)):
                    for i in range(2):
                        coded[side, j, f, i] = enc(a[f, j + 1, z0 + i, pl.ds(ROW0, NR), :], 1.0)

        if k == 0:
            pl.semaphore_wait(barrier, len(around))
            tell(0)
        js = pl.ds(jnp.minimum(tile(k * wide, 1 - core), tile(k * wide + wide - 1, 1 - core)), wide)
        for side, who in ((0, du), (1, dd)):
            send(coded.at[side, js], zbuf.at[side, js], (t, who))
        if k == CH - 1:
            send(a.at[:, inner, depth, pl.ds(ROW0 + NR - 2, 2), :], a.at[:, inner, depth, pl.ds(ROW0 - 2, 2), :], (tu, d))
            send(a.at[:, inner, depth, pl.ds(ROW0, 2), :], a.at[:, inner, depth, pl.ds(ROW0 + NR, 2), :], (td, d))
        if k == CH - 1:
            for z0, z1, wz in ((DZ + 1, 1, du), (2, DZ + 2, dd)):
                for r0, r1, wx in ((ROW0 + NR - 1, ROW0 - 1, tu), (ROW0, ROW0 + NR, td)):
                    send(a.at[:, inner, z0, pl.ds(r0, 1), :], a.at[:, inner, z1, pl.ds(r1, 1), :], (wx, wz))
    layers_in = [copies[2 * k : 2 * k + 2] for k in range(CH)]
    rows_in, corners_in = copies[2 * CH : 2 * CH + 2], copies[2 * CH + 2 :]

    def steps(body, rs):
        lo, hi, step = rs
        n = (hi - lo) // step + 1
        lax.fori_loop(0, n, lambda i, c: body(lo + step * i, c), 0, unroll=n)

    def first(j, zs, rs, outer=()):
        def body(r, carry, zs=zs):
            for z0, nz in zs:
                r0 = ROW0 - 1 + 8 * r
                lane = lax.broadcasted_iota(I32, (nz, 8, 128), 2)
                us, vs = cells(a, 0, j, z0, nz, r0), cells(a, 1, j, z0, nz, r0)
                rows = pl.ds(8 * r, 8)
                b[0, j, pl.ds(z0 - 1, nz), rows, :] = next_u(a, j, z0, nz, r0, us, vs, lane)
                b[1, j, pl.ds(z0 - 1, nz), rows, :] = next_v(a, j, z0, nz, r0, us, vs, lane)
            return carry

        steps(body, rs)
        if outer:
            steps(lambda r, c: body(r, c, outer), (0, 8, 8))
        for s in range(2):

            @pl.when(jnp.logical_not(inx[s]))
            def _():
                for f in range(2):
                    for z0, nz in zs + outer:
                        for k in range(z0 - 1, z0 - 1 + nz):
                            b[f, j, k, pl.ds((NR + 1) * s, 1), :] = jnp.zeros((1, 128), F32)

    def second(f, j, zs, rs=(0, 7, 1), outer=()):
        def body(r, carry, zs=zs):
            for z0, nz in zs:
                r0 = 8 * r + 1
                lane = lax.broadcasted_iota(I32, (nz, 8, 128), 2)
                us, vs = cells(b, 0, j + 1, z0, nz, r0), cells(b, 1, j + 1, z0, nz, r0)
                o[f, j, pl.ds(z0 - 1, nz), pl.ds(8 * r, 8), :] = (next_v if f else next_u)(b, j + 1, z0, nz, r0, us, vs, lane)
            return carry

        steps(body, rs)
        if outer:
            steps(lambda r, c: body(r, c, outer), (0, 7, 7))

    offset = jnp.where(lanes >= 64, 16, 0)

    def shade(j, z0, nz, r):
        keep, total = None, [None] * 3
        for k in range(z0, z0 + nz):
            p = jnp.clip(o[1, j, k, pl.ds(8 * r, 8), :] * 15.0, 0.0, 15.0)
            low = p.astype(I32)
            after = p - low.astype(F32)
            idx, here_ = low + offset, 1.0 - after
            vals = []
            for cc in range(4):
                w = gather(tabs[j, cc], idx)
                x = lax.shift_right_logical(w, 16).astype(F32) * here_ + (w & 65535).astype(F32) * after
                vals.append(x.astype(jnp.bfloat16).astype(F32))
            opacity = vals[3] * AU
            w = opacity if keep is None else opacity * keep
            keep = 1.0 - w if keep is None else keep - w
            for cc in range(3):
                x = vals[cc] * w
                total[cc] = x if total[cc] is None else total[cc] + x
        return total, keep

    def emit(f, j):
        return pltpu.make_async_copy(o.at[f, j], outs[f].at[:, :, pl.ds(j * 128, 128)], osem.at[f, j])

    def middle(j, rs):
        def body(r, carry):
            total, keep = shade(j, 2, 4, r)
            for cc in range(3):
                part[r, j, cc] = total[cc]
            part[r, j, 3] = keep
            return carry

        steps(body, rs)

    @pl.loop(1, LT + 1)
    def _(j):
        first(j, ((3, 6),), (1, 7, 1))


    @pl.loop(0, LT)
    def _(j):
        second(1, j, ((3, 4),), (1, 6, 1))


    hear(0)

    @pl.loop(0, LT, unroll=2)
    def _(j):
        middle(j, (1, 6, 1))

    hear(1)
    for c in rows_in:
        c.wait_recv()
    for s in range(2):

        @pl.when(jnp.logical_not(inx[s]))
        def _():
            @pl.loop(1, LT + 1)
            def _(j):
                for f in range(2):
                    for k in range(2, DZ + 2):
                        a[f, j, k, pl.ds(ROW0 + NR if s else ROW0 - 2, 2), :] = jnp.zeros((2, 128), F32)

    for c in corners_in:
        c.wait_recv()
    for sz in range(2):
        for sx in range(2):

            @pl.when(jnp.logical_not(inz[sz] & inx[sx]))
            def _():
                @pl.loop(1, LT + 1)
                def _(j):
                    for f in range(2):
                        a[f, j, DZ + 2 if sz else 1, pl.ds(ROW0 + NR if sx else ROW0 - 1, 1), :] = jnp.zeros((1, 128), F32)

    def begin(e):
        j = tile(e, core) + 1
        first(j, ((1, 2), (9, 2)), (0, 8, 1), ((3, 6),))
        for s in range(2):

            @pl.when(jnp.logical_not(inz[s]))
            def _():
                for f in range(2):
                    b[f, j, (DZ + 1) * s] = jnp.zeros((NR + 8, 128), F32)

    def finish(e):
        j = tile(e, core)
        second(1, j, ((1, 2), (7, 2)), outer=((3, 4),))
        emit(1, j).start()

        def ends(r, carry):
            front, keep = shade(j, 0, 2, r)
            back, last = shade(j, 6, 2, r)
            mid = part[r, j, 3]
            for cc in range(3):
                part[r, j, cc] = front[cc] + keep * (part[r, j, cc] + mid * back[cc])
            part[r, j, 3] = 1.0 - keep * mid * last
            return carry

        def whole(r, carry):
            total, keep = shade(j, 0, DZ, r)
            for cc in range(3):
                part[r, j, cc] = total[cc]
            part[r, j, 3] = 1.0 - keep
            return carry

        steps(ends, (1, 6, 1))
        steps(whole, (0, 7, 7))

    def put(half):
        for i in range(8):
            for l in range(4):
                for cc in range(4):
                    slots[half, i // 2, cc, pl.ds(2 * l + i % 2, 8, stride=8), :] = part[order[i], 4 * half + l, cc]

    swap = pltpu.make_async_remote_copy(src_ref=away, dst_ref=came, send_sem=cs, recv_sem=cr, device_id=(t, d + 1 - 2 * core), device_id_type=MESH)

    began = done = 0
    for k in range(CH):
        for c in layers_in[k]:
            c.wait_recv()

        @pl.loop(k * wide, (k + 1) * wide)
        def _(e):
            j = tile(e, core)
            for s in range(2):
                for f in range(2):
                    for i in range(2):
                        x = dec(zbuf[s, j, f, i], 1.0)
                        a[f, j + 1, (DZ + 2) * s + i, pl.ds(ROW0, NR), :] = jnp.where(inz[s], x, 0.0)

        ready = (k + 1) * wide
        last = LT if ready == LT else ready - 1
        pl.loop(began, last)(begin)
        began = last
        last = LT if ready == LT else max(began - 1, 0)
        for lo, hi in ((done, min(last, 4)), (max(done, 4), last)):
            if lo < hi:
                pl.loop(lo, hi)(finish)
                if hi == 4:
                    put(1 - core)

                    def pack(i, carry):
                        g, q = i // 4, lax.rem(i, 4)
                        for cc in range(4):
                            away[g, q, cc] = enc(slots[1 - core, g, cc, pl.ds(pl.multiple_of(16 * q, 16), 16), :], TOPS[cc])
                        return carry

                    lax.fori_loop(0, 16, pack, 0, unroll=4)
                    hear(2)
                    swap.start()
        done = last
    put(core)
    swap.wait_recv()

    def join(i, carry):
        g, q = i // 4, lax.rem(i, 4)
        rows = pl.ds(pl.multiple_of(16 * q, 16), 16)
        x = [slots[core, g, cc, rows, :] for cc in range(4)]
        w = [dec(came[g, q, cc], TOPS[cc]) for cc in range(4)]
        ahead = core == 0
        clear = 1.0 - jnp.where(ahead, x[3], w[3])
        for cc in range(4):
            f, s = jnp.where(ahead, x[cc], w[cc]), jnp.where(ahead, w[cc], x[cc])
            pair[g, q, cc] = enc(f + clear * s, 2 * TOPS[cc])
        return carry

    lax.fori_loop(0, 16, join, 0, unroll=4)

    here = z * 4 + y
    owners = [assign[8 * z + p] // 8 for p in range(8)]
    which = []
    for p in range(8):
        n = jnp.int32(0)
        for q in range(p):
            n = n + (owners[q] == owners[p]).astype(I32)
        which.append(jnp.minimum(n, 1))

    def share(k, dz, dy):
        to_z, to_y = lax.rem(z + dz, 4), lax.rem(y + dy, 4)
        return pltpu.make_async_remote_copy(
            src_ref=pair.at[to_z, pair_of(to_y)], dst_ref=got.at[here], send_sem=ps.at[k], recv_sem=pr.at[k],
            device_id=(t, to_z * 8 + to_y * 2 + core), device_id_type=MESH)

    far = sorted(((dz, dy) for dz in range(4) for dy in range(4) if dz or dy), key=lambda w: -min(w[0], 4 - w[0]) - min(w[1], 4 - w[1]))
    shares = [share(k, dz, dy) for k, (dz, dy) in enumerate(far)]
    for c in shares:
        c.start()
    keep_own = pltpu.make_async_copy(pair.at[z, pair_of(y)], got.at[here], lsem)
    keep_own.start()

    hear(3)
    @pl.loop(0, LT)
    def _(j):
        second(0, j, ((1, 8),))
        emit(0, j).start()

    keep_own.wait()
    hear(4)
    for c in shares:
        c.wait_recv()

    def fold(s, carry):
        keep, total = carry
        x = [dec(got[s, cc], 2 * TOPS[cc]) for cc in range(4)]
        total = tuple(total[cc] + x[cc] * keep for cc in range(3))
        return keep - keep * x[3], total

    zero = jnp.zeros((16, 128), F32)
    _, total = lax.fori_loop(0, 16, fold, (zero + 1.0, (zero, zero, zero)), unroll=4)
    for cc in range(3):
        own[cc] = total[cc]
        for h in range(2):
            pick[h, cc] = own[cc, pl.ds(h, 8, stride=2), :]

    for p in range(8):
        red, green, blue = (pick[which[p], cc] for cc in range(3))
        stage[p, 0] = enc(jnp.concatenate([red, green], axis=0), TOP)
        stage[p, 1] = enc(jnp.concatenate([blue, blue], axis=0), TOP)

    hear(5)

    def spread(k):
        p = lax.rem(k + d // 4, 8)
        to = 4 * p + pair_of(y)
        return p, (z == t) & (to == d), pltpu.make_async_remote_copy(
            src_ref=stage.at[p], dst_ref=lines.at[t, core], send_sem=fs.at[k], recv_sem=fr.at[t, core],
            device_id=(z, to), device_id_type=MESH)

    @pl.loop(0, 8)
    def _(k):
        p, self_, c = spread(k)

        @pl.when(jnp.logical_not(self_))
        def _():
            c.start()

        @pl.when(self_)
        def _():
            pltpu.make_async_copy(stage.at[p], lines.at[t, core], fr.at[t, core]).start()

    for k in range(8):
        pltpu.make_async_copy(stage.at[0], lines.at[k // 2, k % 2], fr.at[k // 2, k % 2]).wait()

    w = assign[8 * t + d // 4] // 8
    scale = CU / unit[...]
    for half in range(2):
        x = [dec(lines[w, half, n], TOP) for n in range(2)]
        for cc in range(3):
            x_ = x[cc // 2][8 * (cc % 2) : 8 * (cc % 2) + 8] * scale
            for r in range(2):
                for l in range(4):
                    image[cc, r : r + 1, pl.ds((4 * half + l) * 128, 128)] = x_[4 * r + l : 4 * r + l + 1]

    for c in copies + [swap] + shares:
        c.wait_send()

    @pl.loop(0, 8)
    def _(k):
        p, self_, c = spread(k)

        @pl.when(jnp.logical_not(self_))
        def _():
            c.wait_send()

    for j in range(LT):
        for f in range(2):
            emit(f, j).wait()


def write(u, v, image, u_out, v_out, image_out, sem, isem):
    copies = [pltpu.make_async_copy(image, image_out, isem)]
    for f, (x, y) in enumerate(((u, u_out), (v, v_out))):
        copies += [pltpu.make_async_copy(x.at[k], y.at[k], sem.at[f, k]) for k in range(DZ)]
    for c in copies:
        c.start()
    for c in copies:
        c.wait()


def local(u, v, bricks, color, alpha, assign):
    hbm = pl.BlockSpec(memory_space=pltpu.HBM)
    vmem = pl.BlockSpec(memory_space=pltpu.VMEM)
    free = pl.BlockSpec(memory_space=pl.ANY)
    dma = pltpu.SemaphoreType.DMA
    u, v, image = pl.pallas_call(
        kernel,
        out_shape=(
            jax.ShapeDtypeStruct((DZ, NR, NY), F32),
            jax.ShapeDtypeStruct((DZ, NR, NY), F32),
            jax.ShapeDtypeStruct((3, 2, NY), F32),
        ),
        in_specs=[hbm] * 6,
        out_specs=(free, free, vmem),
        scratch_shapes=[
            pltpu.SMEM((4, 4, 16), I32),
            pltpu.SMEM((32,), I32),
            pltpu.VMEM((3, 4, 16), F32),
            pltpu.VMEM((4, 16), F32),
            pltpu.VMEM((4, 4, 128), I32),
            pltpu.VMEM((8, 128), F32),
            pltpu.VMEM((2, LT + 2, DZ + 4, NR + 16, 128), F32),
            pltpu.VMEM((2, LT + 2, DZ + 2, NR + 8, 128), F32),
            pltpu.VMEM((2, LT, DZ, NR, 128), F32),
            pltpu.VMEM((2, LT, 2, 2, NR, 128), I16),
            pltpu.VMEM((2, LT, 2, 2, NR, 128), I16),
            pltpu.VMEM((LT, 4, 8, 128), I32),
            pltpu.VMEM((NR // 8, LT, 4, 8, 128), F32),
            pltpu.VMEM((2, 4, 4, NR, 128), F32),
            pltpu.VMEM((4, 4, 4, 16, 128), I16),
            pltpu.VMEM((4, 4, 4, 16, 128), I16),
            pltpu.VMEM((4, 4, 4, 16, 128), I16),
            pltpu.VMEM((16, 4, 16, 128), I16),
            pltpu.VMEM((3, 16, 128), F32),
            pltpu.VMEM((2, 3, 8, 128), F32),
            pltpu.VMEM((8, 2, 16, 128), I16),
            pltpu.VMEM((4, 2, 2, 16, 128), I16),
            pltpu.SemaphoreType.REGULAR((6,)),
            dma((4,)), dma((2, LT)), dma((2, LT)),
            dma((6 + 2 * CH,)), dma((6 + 2 * CH,)),
            dma, dma,
            dma((16,)), dma((16,)),
            dma((8,)), dma((4, 2)),
            dma,
        ],
        compiler_params=pltpu.CompilerParams(collective_id=0, has_side_effects=True, vmem_limit_bytes=48 << 20),
        name="reaction_render",
    )(*[pltpu.with_memory_space_constraint(x, pltpu.HBM) for x in (bricks, assign, u, v, jnp.transpose(color, (1, 0, 2)), alpha)])
    return pl.pallas_call(
        write,
        out_shape=(
            jax.ShapeDtypeStruct((DZ, NR, NY), F32),
            jax.ShapeDtypeStruct((DZ, NR, NY), F32),
            jax.ShapeDtypeStruct((3, 2, NY), F32),
        ),
        in_specs=[free] * 3,
        out_specs=(hbm, hbm, hbm),
        scratch_shapes=[dma((2, DZ)), dma],
        compiler_params=pltpu.CompilerParams(vmem_limit_bytes=1 << 20),
        name="write",
    )(u, v, image)


def solution(mesh):
    in_specs = (P("dev", "tile", None), P("dev", "tile", None), P(), P(), P(), P())
    out_specs = (P("dev", "tile", None), P("dev", "tile", None), P(None, ("tile", "dev"), None))
    return jax.shard_map(local, mesh=mesh, in_specs=in_specs, out_specs=out_specs, check_vma=False)
```

```python
import jax
import jax.numpy as jnp
from jax import lax
from jax.experimental import pallas as pl
from jax.experimental.pallas import tpu as pltpu
from jax.sharding import PartitionSpec as P

MESH = pl.DeviceIdType.MESH
I16 = jnp.int16
I32 = jnp.int32
F32 = jnp.float32
DZ, NR, NY = 8, 64, 1024
LT = 8
ROW0 = 8
CU, AU = 2.0**-14, 2.0**-21
STEPS, SHIFT = 65534.0, 32767.0
TOPS = (0.32 / CU, 0.32 / CU, 0.32 / CU, 0.16)
TOP = 2.01 / CU
CH = 4


def enc(x, top):
    return jnp.round(x * (STEPS / top) - SHIFT).astype(I32).astype(I16)


def dec(x, top):
    return (x.astype(I32).astype(F32) + SHIFT) * (top / STEPS)


def gather(tab, idx):
    return jnp.take_along_axis(tab, idx, axis=1, mode="promise_in_bounds")


def cells(ref, f, j, z0, nz, r0):
    return ref[f, j, pl.ds(z0, nz), pl.ds(r0, 8), :]


def neighbours(ref, f, j, z0, nz, r0, c, lanes):
    depth = cells(ref, f, j, z0 - 1, nz, r0) + cells(ref, f, j, z0 + 1, nz, r0)
    row = cells(ref, f, j, z0, nz, r0 - 1) + cells(ref, f, j, z0, nz, r0 + 1)
    left = pltpu.roll(jnp.where(lanes == 127, cells(ref, f, j - 1, z0, nz, r0), c), 1, 2)
    right = pltpu.roll(jnp.where(lanes == 0, cells(ref, f, j + 1, z0, nz, r0), c), 127, 2)
    return depth + row + (left + right)


def next_u(ref, j, z0, nz, r0, u, v, lanes):
    return 0.16 * neighbours(ref, 0, j, z0, nz, r0, u, lanes) - u * v * v + 0.04


def next_v(ref, j, z0, nz, r0, u, v, lanes):
    return 0.08 * neighbours(ref, 1, j, z0, nz, r0, v, lanes) + (0.42 * v + u * v * v)


def kernel(bricks_in, assign_in, u, v, color_in, alpha_in, u_out, v_out, image, bricks, assign, color, alpha, nodes, unit, a, b, o,
           coded, zbuf, tabs, part, slots, away, came, pair, got, own, pick, stage, lines, told, tsem, isem, osem, hs, hr, cs, cr,
           ps, pr, fs, fr, lsem):
    t, d = lax.axis_index("tile"), lax.axis_index("dev")
    nt, nd = lax.axis_size("tile"), lax.axis_size("dev")
    tu, td = lax.rem(t + 1, nt), lax.rem(t + nt - 1, nt)
    du, dd = lax.rem(d + 1, nd), lax.rem(d + nd - 1, nd)
    z, y, core = d // 8, lax.rem(d // 2, 4), lax.rem(d, 2)

    def group_of(zz):
        return lax.rem(zz + nt - t, nt)

    group = group_of(z)

    def pair_of(yy):
        return 2 * (1 - lax.rem(yy, 2)) + yy // 2

    def chip_of(q):
        return 2 * lax.rem(q, 2) + 1 - q // 2

    fields, outs = (u, v), (u_out, v_out)
    inz = (d > 0, d < nd - 1)
    inx = (t > 0, t < nt - 1)

    def fetch(f, j):
        return pltpu.make_async_copy(
            fields[f].at[:, :, pl.ds(j * 128, 128)], a.at[f, j + 1, pl.ds(2, DZ), pl.ds(ROW0, NR), :], isem.at[f, j])

    smalls = [pltpu.make_async_copy(x, y_, tsem.at[n]) for n, (x, y_) in enumerate(
        ((bricks_in, bricks), (assign_in, assign), (color_in, color), (alpha_in, alpha)))]
    for c in smalls:
        c.start()
    def tile(e, who):
        return jnp.where(who == 1, e, LT - 1 - e)

    for e in range(LT):
        for f in range(2):
            fetch(f, tile(e, 1 - core)).start()

    barrier = pltpu.get_barrier_semaphore()

    def greet(who):
        pl.semaphore_signal(barrier, inc=1, device_id=who, device_id_type=MESH)

    around = [(tt, d2) for tt in (td, t, tu) for d2 in (dd, d, du)]
    around.pop(4)
    def chip(zz, yy):
        return (t, lax.rem(zz, 4) * 8 + lax.rem(yy, 4) * 2 + core)

    sides_y = (chip(z, y + 1), chip(z, y + 3))
    sides_z = (chip(z + 1, y), chip(z + 3, y))
    sides_x = ((tu, d), (td, d))
    around += sides_y + sides_z
    for who in around:
        greet(who)

    shown = lax.rem(d, 4)

    rounds = (sides_y, sides_z, sides_z, sides_x, sides_x, ((t, d + 1 - 2 * core),))

    def tell(n):
        for who in rounds[n]:
            pl.semaphore_signal(told.at[n], inc=1, device_id=who, device_id_type=MESH)

    def hear(n):
        pl.semaphore_wait(told.at[n], len(rounds[n]))
        if n + 1 < len(rounds):
            tell(n + 1)

    for c in smalls:
        c.wait()
    largest = color[0]
    for cc in (1, 2):
        largest = jnp.maximum(largest, color[cc])
    largest = jnp.max(jnp.max(largest, axis=0, keepdims=True), axis=1, keepdims=True)
    up = jnp.ones((1, 1), F32)
    for n in (8, 4, 2, 1):
        up = jnp.where(largest * up * 2.0**n <= 2.0, up * 2.0**n, up)
    unit[...] = jnp.broadcast_to(up, (8, 128))
    for cc in range(4):
        for m in range(4):
            row = color[cc, m : m + 1, :] if cc < 3 else alpha[m : m + 1, :]
            nodes[m, cc : cc + 1, 0:16] = jnp.round(row * up * (1 / CU) if cc < 3 else row * (1 / AU)).astype(I32)
    lanes = lax.broadcasted_iota(I32, (8, 128), 1)

    @pl.loop(0, LT)
    def _(j):
        rows = []
        for half in range(2):
            m = bricks[d * DZ // 64, t * NR // 64, 2 * j + half]
            rows.append([jnp.broadcast_to(nodes[m, cc][None], (8, 128)) for cc in range(4)])
        for cc in range(4):
            x = jnp.where(lanes < 16, rows[0][cc], pltpu.roll(rows[1][cc], 16, 1))
            tabs[j, cc] = x * 65536 + pltpu.roll(x, 127, 1)

    order = []
    for g in range(4):
        seen = jnp.int32(0)
        found = [jnp.int32(0), jnp.int32(0)]
        for p in range(8):
            w = assign[8 * g + p]
            mine = (w // 8 == t).astype(I32)
            for h in range(2):
                found[h] = found[h] + mine * (seen == h).astype(I32) * lax.rem(w, 8)
            seen = seen + mine
        order += found

    for ref, nz, nr in ((a, DZ + 4, NR + 16), (b, DZ + 2, NR + 8)):
        for f in range(2):
            for j in (0, LT + 1):

                @pl.loop(0, nz)
                def _(k):
                    ref[f, j, k] = jnp.zeros((nr, 128), F32)

    def send(src, dst, who):
        n = len(copies)
        c = pltpu.make_async_remote_copy(src_ref=src, dst_ref=dst, send_sem=hs.at[n], recv_sem=hr.at[n], device_id=who, device_id_type=MESH)
        c.start()
        copies.append(c)

    wide = LT // CH
    inner, depth = pl.ds(1, LT), pl.ds(2, DZ)
    def layers(k, side):
        js = pl.ds(jnp.minimum(tile(k * wide, 1 - core), tile(k * wide + wide - 1, 1 - core)), wide)
        n = 2 * k + side
        return pltpu.make_async_remote_copy(
            src_ref=coded.at[side, js], dst_ref=zbuf.at[side, js], send_sem=hs.at[n], recv_sem=hr.at[n],
            device_id=(t, (du, dd)[side]), device_id_type=MESH)

    @pl.loop(0, CH)
    def _(k):
        @pl.loop(k * wide, (k + 1) * wide)
        def _(e):
            j = tile(e, 1 - core)
            for f in range(2):
                fetch(f, j).wait()
                for side, z0 in ((0, DZ), (1, 2)):
                    for i in range(2):
                        coded[side, j, f, i] = enc(a[f, j + 1, z0 + i, pl.ds(ROW0, NR), :], 1.0)

        @pl.when(k == 0)
        def _():
            pl.semaphore_wait(barrier, len(around))
            tell(0)

        for side in range(2):
            layers(k, side).start()

    copies = [layers(k, side) for k in range(CH) for side in range(2)]
    send(a.at[:, inner, depth, pl.ds(ROW0 + NR - 2, 2), :], a.at[:, inner, depth, pl.ds(ROW0 - 2, 2), :], (tu, d))
    send(a.at[:, inner, depth, pl.ds(ROW0, 2), :], a.at[:, inner, depth, pl.ds(ROW0 + NR, 2), :], (td, d))
    for z0, z1, wz in ((DZ + 1, 1, du), (2, DZ + 2, dd)):
        for r0, r1, wx in ((ROW0 + NR - 1, ROW0 - 1, tu), (ROW0, ROW0 + NR, td)):
            send(a.at[:, inner, z0, pl.ds(r0, 1), :], a.at[:, inner, z1, pl.ds(r1, 1), :], (wx, wz))
    rows_in, corners_in = copies[2 * CH : 2 * CH + 2], copies[2 * CH + 2 :]

    def steps(body, rs):
        lo, hi, step = rs
        n = (hi - lo) // step + 1
        lax.fori_loop(0, n, lambda i, c: body(lo + step * i, c), 0, unroll=n)

    def first(j, zs, rs, outer=()):
        def body(r, carry, zs=zs):
            for z0, nz, fs in zs:
                r0 = ROW0 - 1 + 8 * r
                lane = lax.broadcasted_iota(I32, (nz, 8, 128), 2)
                us, vs = cells(a, 0, j, z0, nz, r0), cells(a, 1, j, z0, nz, r0)
                for f in fs:
                    b[f, j, pl.ds(z0 - 1, nz), pl.ds(8 * r, 8), :] = (next_v if f else next_u)(a, j, z0, nz, r0, us, vs, lane)
            return carry

        steps(body, rs)
        if outer:
            steps(lambda r, c: body(r, c, outer), (0, 8, 8))
        for s in range(2):

            @pl.when(jnp.logical_not(inx[s]))
            def _():
                for z0, nz, fs in zs + outer:
                    for k in range(z0 - 1, z0 - 1 + nz):
                        for f in fs:
                            b[f, j, k, pl.ds((NR + 1) * s, 1), :] = jnp.zeros((1, 128), F32)

    def second(f, j, zs, rs=(0, 7, 1), outer=()):
        def body(r, carry, zs=zs):
            for z0, nz in zs:
                r0 = 8 * r + 1
                lane = lax.broadcasted_iota(I32, (nz, 8, 128), 2)
                us, vs = cells(b, 0, j + 1, z0, nz, r0), cells(b, 1, j + 1, z0, nz, r0)
                o[f, j, pl.ds(z0 - 1, nz), pl.ds(8 * r, 8), :] = (next_v if f else next_u)(b, j + 1, z0, nz, r0, us, vs, lane)
            return carry

        steps(body, rs)
        if outer:
            steps(lambda r, c: body(r, c, outer), (0, 7, 7))

    offset = jnp.where(lanes >= 64, 16, 0)

    def shade(j, z0, nz, r):
        keep, total = None, [None] * 3
        for k in range(z0, z0 + nz):
            p = jnp.clip(o[1, j, k, pl.ds(8 * r, 8), :] * 15.0, 0.0, 15.0)
            low = p.astype(I32)
            after = p - low.astype(F32)
            idx, here_ = low + offset, 1.0 - after
            vals = []
            for cc in range(4):
                w = gather(tabs[j, cc], idx)
                x = lax.shift_right_logical(w, 16).astype(F32) * here_ + (w & 65535).astype(F32) * after
                vals.append(x.astype(jnp.bfloat16).astype(F32))
            opacity = vals[3] * AU
            w = opacity if keep is None else opacity * keep
            keep = 1.0 - w if keep is None else keep - w
            for cc in range(3):
                x = vals[cc] * w
                total[cc] = x if total[cc] is None else total[cc] + x
        return total, keep

    def emit(f, j):
        return pltpu.make_async_copy(o.at[f, j], outs[f].at[:, :, pl.ds(j * 128, 128)], osem.at[f, j])

    def middle(j, rs):
        def body(r, carry):
            total, keep = shade(j, 2, 4, r)
            for cc in range(3):
                part[r, j, cc] = total[cc]
            part[r, j, 3] = keep
            return carry

        steps(body, rs)

    @pl.loop(1, LT + 1)
    def _(j):
        first(j, ((3, 6, (0, 1)),), (1, 7, 1))


    @pl.loop(0, LT, unroll=2)
    def _(j):
        second(1, j, ((3, 4),), (1, 6, 1))


    hear(0)

    @pl.loop(0, LT, unroll=2)
    def _(j):
        middle(j, (1, 6, 1))

    hear(1)
    for c in rows_in:
        c.wait_recv()
    for s in range(2):

        @pl.when(jnp.logical_not(inx[s]))
        def _():
            @pl.loop(1, LT + 1)
            def _(j):
                for f in range(2):
                    for k in range(2, DZ + 2):
                        a[f, j, k, pl.ds(ROW0 + NR if s else ROW0 - 2, 2), :] = jnp.zeros((2, 128), F32)

    for c in corners_in:
        c.wait_recv()
    for sz in range(2):
        for sx in range(2):

            @pl.when(jnp.logical_not(inz[sz] & inx[sx]))
            def _():
                @pl.loop(1, LT + 1)
                def _(j):
                    for f in range(2):
                        a[f, j, DZ + 2 if sz else 1, pl.ds(ROW0 + NR if sx else ROW0 - 1, 1), :] = jnp.zeros((1, 128), F32)

    def begin(e):
        j = tile(e, core) + 1
        first(j, ((2, 1, (0,)), (9, 1, (0,)), (1, 2, (1,)), (9, 2, (1,))), (0, 8, 1), ((3, 6, (0, 1)),))
        for s in range(2):

            @pl.when(jnp.logical_not(inz[s]))
            def _():
                b[1, j, (DZ + 1) * s] = jnp.zeros((NR + 8, 128), F32)

    def finish(i):
        js = [tile(2 * i + n, core) for n in range(2)]
        for j in js:
            second(1, j, ((1, 2), (7, 2)), outer=((3, 4),))
        for j in js:

            def ends(r, carry):
                front, keep = shade(j, 0, 2, r)
                back, last = shade(j, 6, 2, r)
                mid = part[r, j, 3]
                for cc in range(3):
                    part[r, j, cc] = front[cc] + keep * (part[r, j, cc] + mid * back[cc])
                part[r, j, 3] = 1.0 - keep * mid * last
                return carry

            def whole(r, carry):
                total, keep = shade(j, 0, DZ, r)
                for cc in range(3):
                    part[r, j, cc] = total[cc]
                part[r, j, 3] = 1.0 - keep
                return carry

            steps(ends, (1, 6, 1))
            steps(whole, (0, 7, 7))
        for j in js:
            emit(1, j).start()

    def put(half):
        for i in range(8):
            for l in range(4):
                for cc in range(4):
                    slots[half, i // 2, cc, pl.ds(2 * l + i % 2, 8, stride=8), :] = part[order[i], 4 * half + l, cc]

    swap = pltpu.make_async_remote_copy(src_ref=away, dst_ref=came, send_sem=cs, recv_sem=cr, device_id=(t, d + 1 - 2 * core), device_id_type=MESH)

    @pl.loop(0, CH)
    def _(k):
        for side in range(2):
            layers(k, side).wait_recv()

        @pl.loop(k * wide, (k + 1) * wide)
        def _(e):
            j = tile(e, core)
            for s in range(2):
                for f in range(2):
                    for i in range(2):
                        x = dec(zbuf[s, j, f, i], 1.0)
                        a[f, j + 1, (DZ + 2) * s + i, pl.ds(ROW0, NR), :] = jnp.where(inz[s], x, 0.0)

        end = k == CH - 1
        pl.loop(jnp.maximum(wide * k - 1, 0), jnp.where(end, LT, wide * k + 1))(begin)
        pl.loop(jnp.maximum(k - 1, 0), jnp.where(end, LT // 2, k))(finish)

        @pl.when(k == CH // 2)
        def _():
            put(1 - core)

            def pack(i, carry):
                g, q = i // 4, lax.rem(i, 4)
                for cc in range(4):
                    away[g, q, cc] = enc(slots[1 - core, g, cc, pl.ds(pl.multiple_of(16 * q, 16), 16), :], TOPS[cc])
                return carry

            lax.fori_loop(0, 16, pack, 0, unroll=4)
            hear(2)
            swap.start()

    put(core)
    swap.wait_recv()

    def join(i, carry):
        g, q = i // 4, lax.rem(i, 4)
        rows = pl.ds(pl.multiple_of(16 * q, 16), 16)
        x = [slots[core, g, cc, rows, :] for cc in range(4)]
        w = [dec(came[g, q, cc], TOPS[cc]) for cc in range(4)]
        ahead = core == 0
        clear = 1.0 - jnp.where(ahead, x[3], w[3])
        for cc in range(4):
            f, s = jnp.where(ahead, x[cc], w[cc]), jnp.where(ahead, w[cc], x[cc])
            pair[g, q, cc] = enc(f + clear * s, 2 * TOPS[cc])
        return carry

    lax.fori_loop(0, 16, join, 0, unroll=4)

    here = z * 4 + y
    owners = [assign[8 * group + p] // 8 for p in range(8)]
    which = []
    for p in range(8):
        n = jnp.int32(0)
        for q in range(p):
            n = n + (owners[q] == owners[p]).astype(I32)
        which.append(jnp.minimum(n, 1))

    def share(k, dz, dy):
        to_z, to_y = lax.rem(z + dz, 4), lax.rem(y + dy, 4)
        return pltpu.make_async_remote_copy(
            src_ref=pair.at[group_of(to_z), pair_of(to_y)], dst_ref=got.at[here], send_sem=ps.at[k], recv_sem=pr.at[k],
            device_id=(t, to_z * 8 + to_y * 2 + core), device_id_type=MESH)

    far = sorted(((dz, dy) for dz in range(4) for dy in range(4) if dz or dy), key=lambda w: -min(w[0], 4 - w[0]) - min(w[1], 4 - w[1]))
    shares = [share(k, dz, dy) for k, (dz, dy) in enumerate(far)]
    for c in shares:
        c.start()
    keep_own = pltpu.make_async_copy(pair.at[group, pair_of(y)], got.at[here], lsem)
    keep_own.start()

    hear(3)
    @pl.loop(1, LT + 1)
    def _(j):
        first(j, ((1, 1, (0,)), (DZ + 2, 1, (0,))), (0, 8, 1))
        for s in range(2):

            @pl.when(jnp.logical_not(inz[s]))
            def _():
                b[0, j, (DZ + 1) * s] = jnp.zeros((NR + 8, 128), F32)

    @pl.loop(0, LT)
    def _(j):
        second(0, j, ((1, 8),))
        emit(0, j).start()

    keep_own.wait()
    hear(4)
    for c in shares:
        c.wait_recv()

    def fold(s, carry):
        keep, total = carry
        x = [dec(got[s, cc], 2 * TOPS[cc]) for cc in range(4)]
        total = tuple(total[cc] + x[cc] * keep for cc in range(3))
        return keep - keep * x[3], total

    zero = jnp.zeros((16, 128), F32)
    _, total = lax.fori_loop(0, 16, fold, (zero + 1.0, (zero, zero, zero)), unroll=4)
    for cc in range(3):
        own[cc] = total[cc]
        for h in range(2):
            pick[h, cc] = own[cc, pl.ds(h, 8, stride=2), :]

    for p in range(8):
        red, green, blue = (pick[which[p], cc] for cc in range(3))
        stage[p, 0] = enc(jnp.concatenate([red, green], axis=0), TOP)
        stage[p, 1] = enc(jnp.concatenate([blue, blue], axis=0), TOP)

    hear(5)

    def spread(k):
        p = lax.rem(k + d // 4, 8)
        to = 4 * p + pair_of(y)
        return p, (group == t) & (to == d), pltpu.make_async_remote_copy(
            src_ref=stage.at[p], dst_ref=lines.at[t, core], send_sem=fs.at[k], recv_sem=fr.at[t, core],
            device_id=(group, to), device_id_type=MESH)

    @pl.loop(0, 8)
    def _(k):
        p, self_, c = spread(k)

        @pl.when(jnp.logical_not(self_))
        def _():
            c.start()

        @pl.when(self_)
        def _():
            pltpu.make_async_copy(stage.at[p], lines.at[t, core], fr.at[t, core]).start()

    for k in range(8):
        pltpu.make_async_copy(stage.at[0], lines.at[k // 2, k % 2], fr.at[k // 2, k % 2]).wait()

    w = assign[8 * t + d // 4] // 8
    scale = CU / unit[...]
    for half in range(2):
        x = [dec(lines[w, half, n], TOP) for n in range(2)]
        for cc in range(3):
            x_ = x[cc // 2][8 * (cc % 2) : 8 * (cc % 2) + 8] * scale
            for r in range(2):
                for l in range(4):
                    image[cc, r : r + 1, pl.ds((4 * half + l) * 128, 128)] = x_[4 * r + l : 4 * r + l + 1]

    for c in copies + [swap] + shares:
        c.wait_send()

    @pl.loop(0, 8)
    def _(k):
        p, self_, c = spread(k)

        @pl.when(jnp.logical_not(self_))
        def _():
            c.wait_send()

    for j in range(LT):
        for f in range(2):
            emit(f, j).wait()


def write(u, v, image, u_out, v_out, image_out, sem, isem):
    copies = [pltpu.make_async_copy(image, image_out, isem)]
    for f, (x, y) in enumerate(((u, u_out), (v, v_out))):
        copies += [pltpu.make_async_copy(x.at[k], y.at[k], sem.at[f, k]) for k in range(DZ)]
    for c in copies:
        c.start()
    for c in copies:
        c.wait()


def local(u, v, bricks, color, alpha, assign):
    hbm = pl.BlockSpec(memory_space=pltpu.HBM)
    vmem = pl.BlockSpec(memory_space=pltpu.VMEM)
    free = pl.BlockSpec(memory_space=pl.ANY)
    dma = pltpu.SemaphoreType.DMA
    u, v, image = pl.pallas_call(
        kernel,
        out_shape=(
            jax.ShapeDtypeStruct((DZ, NR, NY), F32),
            jax.ShapeDtypeStruct((DZ, NR, NY), F32),
            jax.ShapeDtypeStruct((3, 2, NY), F32),
        ),
        in_specs=[hbm] * 6,
        out_specs=(free, free, vmem),
        scratch_shapes=[
            pltpu.SMEM((4, 4, 16), I32),
            pltpu.SMEM((32,), I32),
            pltpu.VMEM((3, 4, 16), F32),
            pltpu.VMEM((4, 16), F32),
            pltpu.VMEM((4, 4, 128), I32),
            pltpu.VMEM((8, 128), F32),
            pltpu.VMEM((2, LT + 2, DZ + 4, NR + 16, 128), F32),
            pltpu.VMEM((2, LT + 2, DZ + 2, NR + 8, 128), F32),
            pltpu.VMEM((2, LT, DZ, NR, 128), F32),
            pltpu.VMEM((2, LT, 2, 2, NR, 128), I16),
            pltpu.VMEM((2, LT, 2, 2, NR, 128), I16),
            pltpu.VMEM((LT, 4, 8, 128), I32),
            pltpu.VMEM((NR // 8, LT, 4, 8, 128), F32),
            pltpu.VMEM((2, 4, 4, NR, 128), F32),
            pltpu.VMEM((4, 4, 4, 16, 128), I16),
            pltpu.VMEM((4, 4, 4, 16, 128), I16),
            pltpu.VMEM((4, 4, 4, 16, 128), I16),
            pltpu.VMEM((16, 4, 16, 128), I16),
            pltpu.VMEM((3, 16, 128), F32),
            pltpu.VMEM((2, 3, 8, 128), F32),
            pltpu.VMEM((8, 2, 16, 128), I16),
            pltpu.VMEM((4, 2, 2, 16, 128), I16),
            pltpu.SemaphoreType.REGULAR((6,)),
            dma((4,)), dma((2, LT)), dma((2, LT)),
            dma((6 + 2 * CH,)), dma((6 + 2 * CH,)),
            dma, dma,
            dma((16,)), dma((16,)),
            dma((8,)), dma((4, 2)),
            dma,
        ],
        compiler_params=pltpu.CompilerParams(collective_id=0, has_side_effects=True, vmem_limit_bytes=48 << 20),
        name="reaction_render",
    )(*[pltpu.with_memory_space_constraint(x, pltpu.HBM) for x in (bricks, assign, u, v, jnp.transpose(color, (1, 0, 2)), alpha)])
    return pl.pallas_call(
        write,
        out_shape=(
            jax.ShapeDtypeStruct((DZ, NR, NY), F32),
            jax.ShapeDtypeStruct((DZ, NR, NY), F32),
            jax.ShapeDtypeStruct((3, 2, NY), F32),
        ),
        in_specs=[free] * 3,
        out_specs=(hbm, hbm, hbm),
        scratch_shapes=[dma((2, DZ)), dma],
        compiler_params=pltpu.CompilerParams(vmem_limit_bytes=1 << 20),
        name="write",
    )(u, v, image)


def solution(mesh):
    in_specs = (P("dev", "tile", None), P("dev", "tile", None), P(), P(), P(), P())
    out_specs = (P("dev", "tile", None), P("dev", "tile", None), P(None, ("tile", "dev"), None))
    return jax.shard_map(local, mesh=mesh, in_specs=in_specs, out_specs=out_specs, check_vma=False)
```

```python
import jax
import jax.numpy as jnp
from jax import lax
from jax.experimental import pallas as pl
from jax.experimental.pallas import tpu as pltpu
from jax.sharding import PartitionSpec as P

MESH = pl.DeviceIdType.MESH
I16 = jnp.int16
I32 = jnp.int32
F32 = jnp.float32
DZ, NR, NY = 8, 64, 1024
LT = 8
ROW0 = 8
CU, AU = 2.0**-14, 2.0**-21
STEPS, SHIFT = 65534.0, 32767.0
TOPS = (0.32 / CU, 0.32 / CU, 0.32 / CU, 0.16)
TOP = 2.01 / CU
CH = 4


def enc(x, top):
    return jnp.round(x * (STEPS / top) - SHIFT).astype(I32).astype(I16)


def dec(x, top):
    return (x.astype(I32).astype(F32) + SHIFT) * (top / STEPS)


def gather(tab, idx):
    return jnp.take_along_axis(tab, idx, axis=1, mode="promise_in_bounds")


def cells(ref, f, j, z0, nz, r0):
    return ref[f, j, pl.ds(z0, nz), pl.ds(r0, 8), :]


def neighbours(ref, f, j, z0, nz, r0, c, lanes):
    depth = cells(ref, f, j, z0 - 1, nz, r0) + cells(ref, f, j, z0 + 1, nz, r0)
    row = cells(ref, f, j, z0, nz, r0 - 1) + cells(ref, f, j, z0, nz, r0 + 1)
    left = pltpu.roll(jnp.where(lanes == 127, cells(ref, f, j - 1, z0, nz, r0), c), 1, 2)
    right = pltpu.roll(jnp.where(lanes == 0, cells(ref, f, j + 1, z0, nz, r0), c), 127, 2)
    return depth + row + (left + right)


def next_u(ref, j, z0, nz, r0, u, v, lanes):
    return 0.16 * neighbours(ref, 0, j, z0, nz, r0, u, lanes) - u * v * v + 0.04


def next_v(ref, j, z0, nz, r0, u, v, lanes):
    return 0.08 * neighbours(ref, 1, j, z0, nz, r0, v, lanes) + (0.42 * v + u * v * v)


def kernel(bricks_in, assign_in, u, v, color_in, alpha_in, u_out, v_out, image, bricks, assign, color, alpha, nodes, unit, a, b, o,
           coded, zbuf, tabs, part, slots, away, came, pair, got, own, pick, stage, lines, told, tsem, isem, osem, hs, hr, cs, cr,
           ps, pr, fs, fr, lsem):
    t, d = lax.axis_index("tile"), lax.axis_index("dev")
    nt, nd = lax.axis_size("tile"), lax.axis_size("dev")
    tu, td = lax.rem(t + 1, nt), lax.rem(t + nt - 1, nt)
    du, dd = lax.rem(d + 1, nd), lax.rem(d + nd - 1, nd)
    z, y, core = d // 8, lax.rem(d // 2, 4), lax.rem(d, 2)

    def group_of(zz):
        return lax.rem(zz + nt - t, nt)

    group = group_of(z)

    def pair_of(yy):
        return 2 * (1 - lax.rem(yy, 2)) + yy // 2

    def chip_of(q):
        return 2 * lax.rem(q, 2) + 1 - q // 2

    fields, outs = (u, v), (u_out, v_out)
    inz = (d > 0, d < nd - 1)
    inx = (t > 0, t < nt - 1)

    def fetch(f, j):
        return pltpu.make_async_copy(
            fields[f].at[:, :, pl.ds(j * 128, 128)], a.at[f, j + 1, pl.ds(2, DZ), pl.ds(ROW0, NR), :], isem.at[f, j])

    smalls = [pltpu.make_async_copy(x, y_, tsem.at[n]) for n, (x, y_) in enumerate(
        ((bricks_in, bricks), (assign_in, assign), (color_in, color), (alpha_in, alpha)))]
    for c in smalls:
        c.start()
    def tile(e, who):
        return jnp.where(who == 1, e, LT - 1 - e)

    for e in range(LT):
        for f in range(2):
            fetch(f, tile(e, 1 - core)).start()

    barrier = pltpu.get_barrier_semaphore()

    def greet(who):
        pl.semaphore_signal(barrier, inc=1, device_id=who, device_id_type=MESH)

    around = [(tt, d2) for tt in (td, t, tu) for d2 in (dd, d, du)]
    around.pop(4)
    def chip(zz, yy):
        return (t, lax.rem(zz, 4) * 8 + lax.rem(yy, 4) * 2 + core)

    sides_y = (chip(z, y + 1), chip(z, y + 3))
    sides_z = (chip(z + 1, y), chip(z + 3, y))
    sides_x = ((tu, d), (td, d))
    around += sides_y + sides_z
    for who in around:
        greet(who)

    shown = lax.rem(d, 4)

    rounds = (sides_y, sides_z, sides_z, sides_x, sides_x, ((t, d + 1 - 2 * core),))

    def tell(n):
        for who in rounds[n]:
            pl.semaphore_signal(told.at[n], inc=1, device_id=who, device_id_type=MESH)

    def hear(n):
        pl.semaphore_wait(told.at[n], len(rounds[n]))
        if n + 1 < len(rounds):
            tell(n + 1)

    for ref, nz, nr in ((a, DZ + 4, NR + 16), (b, DZ + 2, NR + 8)):
        for f in range(2):
            for j in (0, LT + 1):

                @pl.loop(0, nz)
                def _(k):
                    ref[f, j, k] = jnp.zeros((nr, 128), F32)

    def send(src, dst, who):
        n = len(copies)
        c = pltpu.make_async_remote_copy(src_ref=src, dst_ref=dst, send_sem=hs.at[n], recv_sem=hr.at[n], device_id=who, device_id_type=MESH)
        c.start()
        copies.append(c)

    wide = LT // CH
    inner, depth = pl.ds(1, LT), pl.ds(2, DZ)
    def layers(k, side):
        js = pl.ds(jnp.minimum(tile(k * wide, 1 - core), tile(k * wide + wide - 1, 1 - core)), wide)
        n = 2 * k + side
        return pltpu.make_async_remote_copy(
            src_ref=coded.at[side, js], dst_ref=zbuf.at[side, js], send_sem=hs.at[n], recv_sem=hr.at[n],
            device_id=(t, (du, dd)[side]), device_id_type=MESH)

    @pl.loop(0, CH)
    def _(k):
        @pl.loop(k * wide, (k + 1) * wide)
        def _(e):
            j = tile(e, 1 - core)
            for f in range(2):
                fetch(f, j).wait()
                for side, z0 in ((0, DZ), (1, 2)):
                    for i in range(2):
                        coded[side, j, f, i] = enc(a[f, j + 1, z0 + i, pl.ds(ROW0, NR), :], 1.0)

        @pl.when(k == 0)
        def _():
            pl.semaphore_wait(barrier, len(around))
            tell(0)

        for side in range(2):
            layers(k, side).start()

    copies = [layers(k, side) for k in range(CH) for side in range(2)]
    send(a.at[:, inner, depth, pl.ds(ROW0 + NR - 2, 2), :], a.at[:, inner, depth, pl.ds(ROW0 - 2, 2), :], (tu, d))
    send(a.at[:, inner, depth, pl.ds(ROW0, 2), :], a.at[:, inner, depth, pl.ds(ROW0 + NR, 2), :], (td, d))
    for z0, z1, wz in ((DZ + 1, 1, du), (2, DZ + 2, dd)):
        for r0, r1, wx in ((ROW0 + NR - 1, ROW0 - 1, tu), (ROW0, ROW0 + NR, td)):
            send(a.at[:, inner, z0, pl.ds(r0, 1), :], a.at[:, inner, z1, pl.ds(r1, 1), :], (wx, wz))
    for c in smalls:
        c.wait()
    largest = color[0]
    for cc in (1, 2):
        largest = jnp.maximum(largest, color[cc])
    largest = jnp.max(jnp.max(largest, axis=0, keepdims=True), axis=1, keepdims=True)
    up = jnp.ones((1, 1), F32)
    for n in (8, 4, 2, 1):
        up = jnp.where(largest * up * 2.0**n <= 2.0, up * 2.0**n, up)
    unit[...] = jnp.broadcast_to(up, (8, 128))
    for cc in range(4):
        for m in range(4):
            row = color[cc, m : m + 1, :] if cc < 3 else alpha[m : m + 1, :]
            nodes[m, cc : cc + 1, 0:16] = jnp.round(row * up * (1 / CU) if cc < 3 else row * (1 / AU)).astype(I32)
    lanes = lax.broadcasted_iota(I32, (8, 128), 1)

    @pl.loop(0, LT)
    def _(j):
        rows = []
        for half in range(2):
            m = bricks[d * DZ // 64, t * NR // 64, 2 * j + half]
            rows.append([jnp.broadcast_to(nodes[m, cc][None], (8, 128)) for cc in range(4)])
        for cc in range(4):
            x = jnp.where(lanes < 16, rows[0][cc], pltpu.roll(rows[1][cc], 16, 1))
            tabs[j, cc] = x * 65536 + pltpu.roll(x, 127, 1)

    order = []
    for g in range(4):
        seen = jnp.int32(0)
        found = [jnp.int32(0), jnp.int32(0)]
        for p in range(8):
            w = assign[8 * g + p]
            mine = (w // 8 == t).astype(I32)
            for h in range(2):
                found[h] = found[h] + mine * (seen == h).astype(I32) * lax.rem(w, 8)
            seen = seen + mine
        order += found

    rows_in, corners_in = copies[2 * CH : 2 * CH + 2], copies[2 * CH + 2 :]

    def steps(body, rs):
        lo, hi, step = rs
        n = (hi - lo) // step + 1
        lax.fori_loop(0, n, lambda i, c: body(lo + step * i, c), 0, unroll=n)

    def first(j, zs, rs, outer=()):
        def body(r, carry, zs=zs):
            for z0, nz, fs in zs:
                r0 = ROW0 - 1 + 8 * r
                lane = lax.broadcasted_iota(I32, (nz, 8, 128), 2)
                us, vs = cells(a, 0, j, z0, nz, r0), cells(a, 1, j, z0, nz, r0)
                for f in fs:
                    b[f, j, pl.ds(z0 - 1, nz), pl.ds(8 * r, 8), :] = (next_v if f else next_u)(a, j, z0, nz, r0, us, vs, lane)
            return carry

        steps(body, rs)
        if outer:
            steps(lambda r, c: body(r, c, outer), (0, 8, 8))
        for s in range(2):

            @pl.when(jnp.logical_not(inx[s]))
            def _():
                for z0, nz, fs in zs + outer:
                    for k in range(z0 - 1, z0 - 1 + nz):
                        for f in fs:
                            b[f, j, k, pl.ds((NR + 1) * s, 1), :] = jnp.zeros((1, 128), F32)

    def second(f, j, zs, rs=(0, 7, 1), outer=()):
        def body(r, carry, zs=zs):
            for z0, nz in zs:
                r0 = 8 * r + 1
                lane = lax.broadcasted_iota(I32, (nz, 8, 128), 2)
                us, vs = cells(b, 0, j + 1, z0, nz, r0), cells(b, 1, j + 1, z0, nz, r0)
                o[f, j, pl.ds(z0 - 1, nz), pl.ds(8 * r, 8), :] = (next_v if f else next_u)(b, j + 1, z0, nz, r0, us, vs, lane)
            return carry

        steps(body, rs)
        if outer:
            steps(lambda r, c: body(r, c, outer), (0, 7, 7))

    offset = jnp.where(lanes >= 64, 16, 0)

    def shade(j, z0, nz, r):
        keep, total = None, [None] * 3
        for k in range(z0, z0 + nz):
            p = jnp.clip(o[1, j, k, pl.ds(8 * r, 8), :] * 15.0, 0.0, 15.0)
            low = p.astype(I32)
            after = p - low.astype(F32)
            idx, here_ = low + offset, 1.0 - after
            vals = []
            for cc in range(4):
                w = gather(tabs[j, cc], idx)
                x = lax.shift_right_logical(w, 16).astype(F32) * here_ + (w & 65535).astype(F32) * after
                vals.append(x.astype(jnp.bfloat16).astype(F32))
            opacity = vals[3] * AU
            w = opacity if keep is None else opacity * keep
            keep = 1.0 - w if keep is None else keep - w
            for cc in range(3):
                x = vals[cc] * w
                total[cc] = x if total[cc] is None else total[cc] + x
        return total, keep

    def emit(f, j):
        return pltpu.make_async_copy(o.at[f, j], outs[f].at[:, :, pl.ds(j * 128, 128)], osem.at[f, j])

    def middle(j, rs):
        def body(r, carry):
            total, keep = shade(j, 2, 4, r)
            for cc in range(3):
                part[r, j, cc] = total[cc]
            part[r, j, 3] = keep
            return carry

        steps(body, rs)

    @pl.loop(1, LT + 1)
    def _(j):
        first(j, ((3, 6, (0, 1)),), (1, 7, 1))


    @pl.loop(0, LT, unroll=2)
    def _(j):
        second(1, j, ((3, 4),), (1, 6, 1))


    hear(0)

    @pl.loop(0, LT, unroll=2)
    def _(j):
        middle(j, (1, 6, 1))

    hear(1)
    for c in rows_in:
        c.wait_recv()
    for s in range(2):

        @pl.when(jnp.logical_not(inx[s]))
        def _():
            @pl.loop(1, LT + 1)
            def _(j):
                for f in range(2):
                    for k in range(2, DZ + 2):
                        a[f, j, k, pl.ds(ROW0 + NR if s else ROW0 - 2, 2), :] = jnp.zeros((2, 128), F32)

    for c in corners_in:
        c.wait_recv()
    for sz in range(2):
        for sx in range(2):

            @pl.when(jnp.logical_not(inz[sz] & inx[sx]))
            def _():
                @pl.loop(1, LT + 1)
                def _(j):
                    for f in range(2):
                        a[f, j, DZ + 2 if sz else 1, pl.ds(ROW0 + NR if sx else ROW0 - 1, 1), :] = jnp.zeros((1, 128), F32)

    def begin(e):
        j = tile(e, core) + 1
        first(j, ((2, 1, (0,)), (9, 1, (0,)), (1, 2, (1,)), (9, 2, (1,))), (0, 8, 1), ((3, 6, (0, 1)),))
        for s in range(2):

            @pl.when(jnp.logical_not(inz[s]))
            def _():
                b[1, j, (DZ + 1) * s] = jnp.zeros((NR + 8, 128), F32)

    def finish(i):
        js = [tile(2 * i + n, core) for n in range(2)]
        for j in js:
            second(1, j, ((1, 2), (7, 2)), outer=((3, 4),))
        for j in js:

            def ends(r, carry):
                front, keep = shade(j, 0, 2, r)
                back, last = shade(j, 6, 2, r)
                mid = part[r, j, 3]
                for cc in range(3):
                    part[r, j, cc] = front[cc] + keep * (part[r, j, cc] + mid * back[cc])
                part[r, j, 3] = 1.0 - keep * mid * last
                return carry

            def whole(r, carry):
                total, keep = shade(j, 0, DZ, r)
                for cc in range(3):
                    part[r, j, cc] = total[cc]
                part[r, j, 3] = 1.0 - keep
                return carry

            steps(ends, (1, 6, 1))
            steps(whole, (0, 7, 7))
        for j in js:
            emit(1, j).start()

    def put(half):
        for i in range(8):
            for l in range(4):
                for cc in range(4):
                    slots[half, i // 2, cc, pl.ds(2 * l + i % 2, 8, stride=8), :] = part[order[i], 4 * half + l, cc]

    swap = pltpu.make_async_remote_copy(src_ref=away, dst_ref=came, send_sem=cs, recv_sem=cr, device_id=(t, d + 1 - 2 * core), device_id_type=MESH)

    @pl.loop(0, CH)
    def _(k):
        for side in range(2):
            layers(k, side).wait_recv()

        @pl.loop(k * wide, (k + 1) * wide)
        def _(e):
            j = tile(e, core)
            for s in range(2):
                for f in range(2):
                    for i in range(2):
                        x = dec(zbuf[s, j, f, i], 1.0)
                        a[f, j + 1, (DZ + 2) * s + i, pl.ds(ROW0, NR), :] = jnp.where(inz[s], x, 0.0)

        end = k == CH - 1
        pl.loop(jnp.maximum(wide * k - 1, 0), jnp.where(end, LT, wide * k + 1))(begin)
        pl.loop(jnp.maximum(k - 1, 0), jnp.where(end, LT // 2, k))(finish)

        @pl.when(k == CH // 2)
        def _():
            put(1 - core)

            def pack(i, carry):
                g, q = i // 4, lax.rem(i, 4)
                for cc in range(4):
                    away[g, q, cc] = enc(slots[1 - core, g, cc, pl.ds(pl.multiple_of(16 * q, 16), 16), :], TOPS[cc])
                return carry

            lax.fori_loop(0, 16, pack, 0, unroll=4)
            hear(2)
            swap.start()

    put(core)
    swap.wait_recv()

    def join(i, carry):
        g, q = i // 4, lax.rem(i, 4)
        rows = pl.ds(pl.multiple_of(16 * q, 16), 16)
        x = [slots[core, g, cc, rows, :] for cc in range(4)]
        w = [dec(came[g, q, cc], TOPS[cc]) for cc in range(4)]
        ahead = core == 0
        clear = 1.0 - jnp.where(ahead, x[3], w[3])
        for cc in range(4):
            f, s = jnp.where(ahead, x[cc], w[cc]), jnp.where(ahead, w[cc], x[cc])
            pair[g, q, cc] = enc(f + clear * s, 2 * TOPS[cc])
        return carry

    lax.fori_loop(0, 16, join, 0, unroll=4)

    here = z * 4 + y
    owners = [assign[8 * group + p] // 8 for p in range(8)]
    which = []
    for p in range(8):
        n = jnp.int32(0)
        for q in range(p):
            n = n + (owners[q] == owners[p]).astype(I32)
        which.append(jnp.minimum(n, 1))

    def share(k, dz, dy):
        to_z, to_y = lax.rem(z + dz, 4), lax.rem(y + dy, 4)
        return pltpu.make_async_remote_copy(
            src_ref=pair.at[group_of(to_z), pair_of(to_y)], dst_ref=got.at[here], send_sem=ps.at[k], recv_sem=pr.at[k],
            device_id=(t, to_z * 8 + to_y * 2 + core), device_id_type=MESH)

    far = sorted(((dz, dy) for dz in range(4) for dy in range(4) if dz or dy), key=lambda w: -min(w[0], 4 - w[0]) - min(w[1], 4 - w[1]))
    shares = [share(k, dz, dy) for k, (dz, dy) in enumerate(far)]
    for c in shares:
        c.start()
    keep_own = pltpu.make_async_copy(pair.at[group, pair_of(y)], got.at[here], lsem)
    keep_own.start()

    hear(3)
    @pl.loop(1, LT + 1)
    def _(j):
        first(j, ((1, 1, (0,)), (DZ + 2, 1, (0,))), (0, 8, 1))
        for s in range(2):

            @pl.when(jnp.logical_not(inz[s]))
            def _():
                b[0, j, (DZ + 1) * s] = jnp.zeros((NR + 8, 128), F32)

    @pl.loop(0, LT)
    def _(j):
        second(0, j, ((1, 8),))
        emit(0, j).start()

    keep_own.wait()
    hear(4)
    for c in shares:
        c.wait_recv()

    def fold(s, carry):
        keep, total = carry
        x = [dec(got[s, cc], 2 * TOPS[cc]) for cc in range(4)]
        total = tuple(total[cc] + x[cc] * keep for cc in range(3))
        return keep - keep * x[3], total

    zero = jnp.zeros((16, 128), F32)
    _, total = lax.fori_loop(0, 16, fold, (zero + 1.0, (zero, zero, zero)), unroll=4)
    for cc in range(3):
        own[cc, 0:16] = total[cc]
        for h in range(2):
            pick[h, cc] = own[cc, pl.ds(h, 8, stride=2), :]

    for p in range(8):
        red, green, blue = (pick[which[p], cc] for cc in range(3))
        stage[p, 0] = enc(jnp.concatenate([red, green], axis=0), TOP)
        stage[p, 1] = enc(jnp.concatenate([blue, blue], axis=0), TOP)

    hear(5)

    def spread(k):
        p = lax.rem(k + d // 4, 8)
        to = 4 * p + pair_of(y)
        return p, (group == t) & (to == d), pltpu.make_async_remote_copy(
            src_ref=stage.at[p], dst_ref=lines.at[t, core], send_sem=fs.at[k], recv_sem=fr.at[t, core],
            device_id=(group, to), device_id_type=MESH)

    @pl.loop(0, 8)
    def _(k):
        p, self_, c = spread(k)

        @pl.when(jnp.logical_not(self_))
        def _():
            c.start()

        @pl.when(self_)
        def _():
            pltpu.make_async_copy(stage.at[p], lines.at[t, core], fr.at[t, core]).start()

    for k in range(8):
        pltpu.make_async_copy(stage.at[0], lines.at[k // 2, k % 2], fr.at[k // 2, k % 2]).wait()

    w = assign[8 * t + d // 4] // 8
    scale = CU / unit[...]
    for half in range(2):
        x = [dec(lines[w, half, n], TOP) for n in range(2)]
        for cc in range(3):
            x_ = x[cc // 2][8 * (cc % 2) : 8 * (cc % 2) + 8] * scale
            for r in range(2):
                for l in range(4):
                    image[cc, r : r + 1, pl.ds((4 * half + l) * 128, 128)] = x_[4 * r + l : 4 * r + l + 1]

    for c in copies + [swap] + shares:
        c.wait_send()

    @pl.loop(0, 8)
    def _(k):
        p, self_, c = spread(k)

        @pl.when(jnp.logical_not(self_))
        def _():
            c.wait_send()

    for j in range(LT):
        for f in range(2):
            emit(f, j).wait()


def write(u, v, image, u_out, v_out, image_out, sem, isem):
    copies = [pltpu.make_async_copy(image, image_out, isem)]
    for f, (x, y) in enumerate(((u, u_out), (v, v_out))):
        copies += [pltpu.make_async_copy(x.at[k], y.at[k], sem.at[f, k]) for k in range(DZ)]
    for c in copies:
        c.start()
    for c in copies:
        c.wait()


def local(u, v, bricks, color, alpha, assign):
    hbm = pl.BlockSpec(memory_space=pltpu.HBM)
    vmem = pl.BlockSpec(memory_space=pltpu.VMEM)
    free = pl.BlockSpec(memory_space=pl.ANY)
    dma = pltpu.SemaphoreType.DMA
    u, v, image = pl.pallas_call(
        kernel,
        out_shape=(
            jax.ShapeDtypeStruct((DZ, NR, NY), F32),
            jax.ShapeDtypeStruct((DZ, NR, NY), F32),
            jax.ShapeDtypeStruct((3, 2, NY), F32),
        ),
        in_specs=[hbm] * 6,
        out_specs=(free, free, vmem),
        scratch_shapes=[
            pltpu.SMEM((4, 4, 16), I32),
            pltpu.SMEM((32,), I32),
            pltpu.VMEM((3, 4, 16), F32),
            pltpu.VMEM((4, 16), F32),
            pltpu.VMEM((4, 4, 128), I32),
            pltpu.VMEM((8, 128), F32),
            pltpu.VMEM((2, LT + 2, DZ + 4, NR + 16, 128), F32),
            pltpu.VMEM((2, LT + 2, DZ + 2, NR + 8, 128), F32),
            pltpu.VMEM((2, LT, DZ, NR, 128), F32),
            pltpu.VMEM((2, LT, 2, 2, NR, 128), I16),
            pltpu.VMEM((2, LT, 2, 2, NR, 128), I16),
            pltpu.VMEM((LT, 4, 8, 128), I32),
            pltpu.VMEM((NR // 8, LT, 4, 8, 128), F32),
            pltpu.VMEM((2, 4, 4, NR + 8, 128), F32),
            pltpu.VMEM((4, 4, 4, 16, 128), I16),
            pltpu.VMEM((4, 4, 4, 16, 128), I16),
            pltpu.VMEM((4, 4, 4, 16, 128), I16),
            pltpu.VMEM((16, 4, 16, 128), I16),
            pltpu.VMEM((3, 24, 128), F32),
            pltpu.VMEM((2, 3, 8, 128), F32),
            pltpu.VMEM((8, 2, 16, 128), I16),
            pltpu.VMEM((4, 2, 2, 16, 128), I16),
            pltpu.SemaphoreType.REGULAR((6,)),
            dma((4,)), dma((2, LT)), dma((2, LT)),
            dma((6 + 2 * CH,)), dma((6 + 2 * CH,)),
            dma, dma,
            dma((16,)), dma((16,)),
            dma((8,)), dma((4, 2)),
            dma,
        ],
        compiler_params=pltpu.CompilerParams(collective_id=0, has_side_effects=True, vmem_limit_bytes=48 << 20),
        name="reaction_render",
    )(*[pltpu.with_memory_space_constraint(x, pltpu.HBM) for x in (bricks, assign, u, v, jnp.transpose(color, (1, 0, 2)), alpha)])
    return pl.pallas_call(
        write,
        out_shape=(
            jax.ShapeDtypeStruct((DZ, NR, NY), F32),
            jax.ShapeDtypeStruct((DZ, NR, NY), F32),
            jax.ShapeDtypeStruct((3, 2, NY), F32),
        ),
        in_specs=[free] * 3,
        out_specs=(hbm, hbm, hbm),
        scratch_shapes=[dma((2, DZ)), dma],
        compiler_params=pltpu.CompilerParams(vmem_limit_bytes=1 << 20),
        name="write",
    )(u, v, image)


def solution(mesh):
    in_specs = (P("dev", "tile", None), P("dev", "tile", None), P(), P(), P(), P())
    out_specs = (P("dev", "tile", None), P("dev", "tile", None), P(None, ("tile", "dev"), None))
    return jax.shard_map(local, mesh=mesh, in_specs=in_specs, out_specs=out_specs, check_vma=False)
```

```python
import jax
import jax.numpy as jnp
from jax import lax
from jax.experimental import pallas as pl
from jax.experimental.pallas import tpu as pltpu
from jax.sharding import PartitionSpec as P

MESH = pl.DeviceIdType.MESH
I16 = jnp.int16
I32 = jnp.int32
F32 = jnp.float32
DZ, NR, NY = 8, 64, 1024
LT = 8
ROW0 = 8
CU, AU = 2.0**-14, 2.0**-21
MID = (0.6, 0.5)
STEPS, SHIFT = 65534.0, 32767.0
TOPS = (0.32 / CU, 0.32 / CU, 0.32 / CU, 0.16)
TOP = 2.01 / CU
CH = 4


def enc(x, top):
    return jnp.round(x * (STEPS / top) - SHIFT).astype(I32).astype(I16)


def dec(x, top):
    return (x.astype(I32).astype(F32) + SHIFT) * (top / STEPS)


def gather(tab, idx):
    return jnp.take_along_axis(tab, idx, axis=1, mode="promise_in_bounds")


def cells(ref, f, j, z0, nz, r0):
    return ref[f, j, pl.ds(z0, nz), pl.ds(r0, 8), :]


def neighbours(ref, f, j, z0, nz, r0, c, lanes):
    depth = cells(ref, f, j, z0 - 1, nz, r0) + cells(ref, f, j, z0 + 1, nz, r0)
    row = cells(ref, f, j, z0, nz, r0 - 1) + cells(ref, f, j, z0, nz, r0 + 1)
    left = pltpu.roll(jnp.where(lanes == 127, cells(ref, f, j - 1, z0, nz, r0), c), 1, 2)
    right = pltpu.roll(jnp.where(lanes == 0, cells(ref, f, j + 1, z0, nz, r0), c), 127, 2)
    return depth + row + (left + right)


def next_u(ref, j, z0, nz, r0, u, v, lanes):
    return 0.16 * neighbours(ref, 0, j, z0, nz, r0, u, lanes) - u * v * v + 0.04


def next_v(ref, j, z0, nz, r0, u, v, lanes):
    return 0.08 * neighbours(ref, 1, j, z0, nz, r0, v, lanes) + (0.42 * v + u * v * v)


def kernel(bricks_in, assign_in, u, v, color_in, alpha_in, u_out, v_out, image, bricks, assign, color, alpha, nodes, unit, a, b, o,
           coded, zbuf, tabs, part, slots, away, came, pair, got, own, pick, stage, lines, told, tsem, isem, osem, hs, hr, cs, cr,
           ps, pr, fs, fr, lsem):
    t, d = lax.axis_index("tile"), lax.axis_index("dev")
    nt, nd = lax.axis_size("tile"), lax.axis_size("dev")
    tu, td = lax.rem(t + 1, nt), lax.rem(t + nt - 1, nt)
    du, dd = lax.rem(d + 1, nd), lax.rem(d + nd - 1, nd)
    z, y, core = d // 8, lax.rem(d // 2, 4), lax.rem(d, 2)

    def group_of(zz):
        return lax.rem(zz + nt - t, nt)

    group = group_of(z)

    def pair_of(yy):
        return 2 * (1 - lax.rem(yy, 2)) + yy // 2

    def chip_of(q):
        return 2 * lax.rem(q, 2) + 1 - q // 2

    fields, outs = (u, v), (u_out, v_out)
    inz = (d > 0, d < nd - 1)
    inx = (t > 0, t < nt - 1)

    def fetch(f, j):
        return pltpu.make_async_copy(
            fields[f].at[:, :, pl.ds(j * 128, 128)], a.at[f, j + 1, pl.ds(2, DZ), pl.ds(ROW0, NR), :], isem.at[f, j])

    smalls = [pltpu.make_async_copy(x, y_, tsem.at[n]) for n, (x, y_) in enumerate(
        ((bricks_in, bricks), (assign_in, assign), (color_in, color), (alpha_in, alpha)))]
    for c in smalls:
        c.start()
    def tile(e, who):
        return jnp.where(who == 1, e, LT - 1 - e)

    for e in range(LT):
        for f in range(2):
            fetch(f, tile(e, 1 - core)).start()

    barrier = pltpu.get_barrier_semaphore()

    def greet(who):
        pl.semaphore_signal(barrier, inc=1, device_id=who, device_id_type=MESH)

    around = [(tt, d2) for tt in (td, t, tu) for d2 in (dd, d, du)]
    around.pop(4)
    def chip(zz, yy):
        return (t, lax.rem(zz, 4) * 8 + lax.rem(yy, 4) * 2 + core)

    sides_y = (chip(z, y + 1), chip(z, y + 3))
    sides_z = (chip(z + 1, y), chip(z + 3, y))
    sides_x = ((tu, d), (td, d))
    around += sides_y + sides_z
    for who in around:
        greet(who)

    shown = lax.rem(d, 4)

    rounds = (sides_y, sides_z, sides_z, sides_x, sides_x, ((t, d + 1 - 2 * core),))

    def tell(n):
        for who in rounds[n]:
            pl.semaphore_signal(told.at[n], inc=1, device_id=who, device_id_type=MESH)

    def hear(n):
        pl.semaphore_wait(told.at[n], len(rounds[n]))
        if n + 1 < len(rounds):
            tell(n + 1)

    for ref, nz, nr in ((a, DZ + 4, NR + 16), (b, DZ + 2, NR + 8)):
        for f in range(2):
            for j in (0, LT + 1):

                @pl.loop(0, nz)
                def _(k):
                    ref[f, j, k] = jnp.zeros((nr, 128), F32)

    def send(src, dst, who):
        n = len(copies)
        c = pltpu.make_async_remote_copy(src_ref=src, dst_ref=dst, send_sem=hs.at[n], recv_sem=hr.at[n], device_id=who, device_id_type=MESH)
        c.start()
        copies.append(c)

    wide = LT // CH
    inner, depth = pl.ds(1, LT), pl.ds(2, DZ)
    def layers(k, side):
        js = pl.ds(jnp.minimum(tile(k * wide, 1 - core), tile(k * wide + wide - 1, 1 - core)), wide)
        n = 2 * k + side
        return pltpu.make_async_remote_copy(
            src_ref=coded.at[side, js], dst_ref=zbuf.at[side, js], send_sem=hs.at[n], recv_sem=hr.at[n],
            device_id=(t, (du, dd)[side]), device_id_type=MESH)

    @pl.loop(0, CH)
    def _(k):
        @pl.loop(k * wide, (k + 1) * wide)
        def _(e):
            j = tile(e, 1 - core)
            for f in range(2):
                fetch(f, j).wait()
                for side, z0 in ((0, DZ), (1, 2)):
                    for i in range(2):
                        coded[side, j, f, i] = (a[f, j + 1, z0 + i, pl.ds(ROW0, NR), :] - MID[f]).astype(jnp.bfloat16)

        @pl.when(k == 0)
        def _():
            pl.semaphore_wait(barrier, len(around))
            tell(0)

        for side in range(2):
            layers(k, side).start()

    copies = [layers(k, side) for k in range(CH) for side in range(2)]
    send(a.at[:, inner, depth, pl.ds(ROW0 + NR - 2, 2), :], a.at[:, inner, depth, pl.ds(ROW0 - 2, 2), :], (tu, d))
    send(a.at[:, inner, depth, pl.ds(ROW0, 2), :], a.at[:, inner, depth, pl.ds(ROW0 + NR, 2), :], (td, d))
    for z0, z1, wz in ((DZ + 1, 1, du), (2, DZ + 2, dd)):
        for r0, r1, wx in ((ROW0 + NR - 1, ROW0 - 1, tu), (ROW0, ROW0 + NR, td)):
            send(a.at[:, inner, z0, pl.ds(r0, 1), :], a.at[:, inner, z1, pl.ds(r1, 1), :], (wx, wz))
    for c in smalls:
        c.wait()
    largest = color[0]
    for cc in (1, 2):
        largest = jnp.maximum(largest, color[cc])
    largest = jnp.max(jnp.max(largest, axis=0, keepdims=True), axis=1, keepdims=True)
    up = jnp.ones((1, 1), F32)
    for n in (8, 4, 2, 1):
        up = jnp.where(largest * up * 2.0**n <= 2.0, up * 2.0**n, up)
    unit[...] = jnp.broadcast_to(up, (8, 128))
    for cc in range(4):
        for m in range(4):
            row = color[cc, m : m + 1, :] if cc < 3 else alpha[m : m + 1, :]
            nodes[m, cc : cc + 1, 0:16] = jnp.round(row * up * (1 / CU) if cc < 3 else row * (1 / AU)).astype(I32)
    lanes = lax.broadcasted_iota(I32, (8, 128), 1)

    @pl.loop(0, LT)
    def _(j):
        rows = []
        for half in range(2):
            m = bricks[d * DZ // 64, t * NR // 64, 2 * j + half]
            rows.append([jnp.broadcast_to(nodes[m, cc][None], (8, 128)) for cc in range(4)])
        for cc in range(4):
            x = jnp.where(lanes < 16, rows[0][cc], pltpu.roll(rows[1][cc], 16, 1))
            tabs[j, cc] = x * 65536 + pltpu.roll(x, 127, 1)

    order = []
    for g in range(4):
        seen = jnp.int32(0)
        found = [jnp.int32(0), jnp.int32(0)]
        for p in range(8):
            w = assign[8 * g + p]
            mine = (w // 8 == t).astype(I32)
            for h in range(2):
                found[h] = found[h] + mine * (seen == h).astype(I32) * lax.rem(w, 8)
            seen = seen + mine
        order += found

    rows_in, corners_in = copies[2 * CH : 2 * CH + 2], copies[2 * CH + 2 :]

    def steps(body, rs):
        lo, hi, step = rs
        n = (hi - lo) // step + 1
        lax.fori_loop(0, n, lambda i, c: body(lo + step * i, c), 0, unroll=n)

    def first(j, zs, rs, outer=()):
        def body(r, carry, zs=zs):
            for z0, nz, fs in zs:
                r0 = ROW0 - 1 + 8 * r
                lane = lax.broadcasted_iota(I32, (nz, 8, 128), 2)
                us, vs = cells(a, 0, j, z0, nz, r0), cells(a, 1, j, z0, nz, r0)
                for f in fs:
                    b[f, j, pl.ds(z0 - 1, nz), pl.ds(8 * r, 8), :] = (next_v if f else next_u)(a, j, z0, nz, r0, us, vs, lane)
            return carry

        steps(body, rs)
        if outer:
            steps(lambda r, c: body(r, c, outer), (0, 8, 8))
        for s in range(2):

            @pl.when(jnp.logical_not(inx[s]))
            def _():
                for z0, nz, fs in zs + outer:
                    for k in range(z0 - 1, z0 - 1 + nz):
                        for f in fs:
                            b[f, j, k, pl.ds((NR + 1) * s, 1), :] = jnp.zeros((1, 128), F32)

    def second(f, j, zs, rs=(0, 7, 1), outer=()):
        def body(r, carry, zs=zs):
            for z0, nz in zs:
                r0 = 8 * r + 1
                lane = lax.broadcasted_iota(I32, (nz, 8, 128), 2)
                us, vs = cells(b, 0, j + 1, z0, nz, r0), cells(b, 1, j + 1, z0, nz, r0)
                o[f, j, pl.ds(z0 - 1, nz), pl.ds(8 * r, 8), :] = (next_v if f else next_u)(b, j + 1, z0, nz, r0, us, vs, lane)
            return carry

        steps(body, rs)
        if outer:
            steps(lambda r, c: body(r, c, outer), (0, 7, 7))

    offset = jnp.where(lanes >= 64, 16, 0)

    def shade(j, z0, nz, r):
        keep, total = None, [None] * 3
        for k in range(z0, z0 + nz):
            p = jnp.clip(o[1, j, k, pl.ds(8 * r, 8), :] * 15.0, 0.0, 15.0)
            low = p.astype(I32)
            after = p - low.astype(F32)
            idx, here_ = low + offset, 1.0 - after
            vals = []
            for cc in range(4):
                w = gather(tabs[j, cc], idx)
                x = lax.shift_right_logical(w, 16).astype(F32) * here_ + (w & 65535).astype(F32) * after
                vals.append(x.astype(jnp.bfloat16).astype(F32))
            opacity = vals[3] * AU
            w = opacity if keep is None else opacity * keep
            keep = 1.0 - w if keep is None else keep - w
            for cc in range(3):
                x = vals[cc] * w
                total[cc] = x if total[cc] is None else total[cc] + x
        return total, keep

    def emit(f, j):
        return pltpu.make_async_copy(o.at[f, j], outs[f].at[:, :, pl.ds(j * 128, 128)], osem.at[f, j])

    def middle(j, rs):
        def body(r, carry):
            total, keep = shade(j, 2, 4, r)
            for cc in range(3):
                part[r, j, cc] = total[cc]
            part[r, j, 3] = keep
            return carry

        steps(body, rs)

    @pl.loop(1, LT + 1)
    def _(j):
        first(j, ((3, 6, (0, 1)),), (1, 7, 1))


    @pl.loop(0, LT, unroll=4)
    def _(j):
        second(1, j, ((3, 4),), (1, 6, 1))


    hear(0)

    @pl.loop(0, LT, unroll=4)
    def _(j):
        middle(j, (1, 6, 1))

    hear(1)
    for c in rows_in:
        c.wait_recv()
    for s in range(2):

        @pl.when(jnp.logical_not(inx[s]))
        def _():
            @pl.loop(1, LT + 1)
            def _(j):
                for f in range(2):
                    for k in range(2, DZ + 2):
                        a[f, j, k, pl.ds(ROW0 + NR if s else ROW0 - 2, 2), :] = jnp.zeros((2, 128), F32)

    for c in corners_in:
        c.wait_recv()
    for sz in range(2):
        for sx in range(2):

            @pl.when(jnp.logical_not(inz[sz] & inx[sx]))
            def _():
                @pl.loop(1, LT + 1)
                def _(j):
                    for f in range(2):
                        a[f, j, DZ + 2 if sz else 1, pl.ds(ROW0 + NR if sx else ROW0 - 1, 1), :] = jnp.zeros((1, 128), F32)

    def begin(e):
        j = tile(e, core) + 1
        first(j, ((2, 1, (0,)), (9, 1, (0,)), (1, 2, (1,)), (9, 2, (1,))), (0, 8, 1), ((3, 6, (0, 1)),))
        for s in range(2):

            @pl.when(jnp.logical_not(inz[s]))
            def _():
                b[1, j, (DZ + 1) * s] = jnp.zeros((NR + 8, 128), F32)

    def finish(i):
        js = [tile(2 * i + n, core) for n in range(2)]
        for j in js:
            second(1, j, ((1, 2), (7, 2)), outer=((3, 4),))
        for j in js:

            def ends(r, carry):
                front, keep = shade(j, 0, 2, r)
                back, last = shade(j, 6, 2, r)
                mid = part[r, j, 3]
                for cc in range(3):
                    part[r, j, cc] = front[cc] + keep * (part[r, j, cc] + mid * back[cc])
                part[r, j, 3] = 1.0 - keep * mid * last
                return carry

            def whole(r, carry):
                total, keep = shade(j, 0, DZ, r)
                for cc in range(3):
                    part[r, j, cc] = total[cc]
                part[r, j, 3] = 1.0 - keep
                return carry

            steps(ends, (1, 6, 1))
            steps(whole, (0, 7, 7))
        for j in js:
            emit(1, j).start()

    def put(half):
        for i in range(8):
            for l in range(4):
                for cc in range(4):
                    slots[half, i // 2, cc, pl.ds(2 * l + i % 2, 8, stride=8), :] = part[order[i], 4 * half + l, cc]

    swap = pltpu.make_async_remote_copy(src_ref=away, dst_ref=came, send_sem=cs, recv_sem=cr, device_id=(t, d + 1 - 2 * core), device_id_type=MESH)

    @pl.loop(0, CH)
    def _(k):
        for side in range(2):
            layers(k, side).wait_recv()

        @pl.loop(k * wide, (k + 1) * wide)
        def _(e):
            j = tile(e, core)
            for s in range(2):
                for f in range(2):
                    for i in range(2):
                        x = zbuf[s, j, f, i].astype(F32) + MID[f]
                        a[f, j + 1, (DZ + 2) * s + i, pl.ds(ROW0, NR), :] = jnp.where(inz[s], x, 0.0)

        end = k == CH - 1
        pl.loop(jnp.maximum(wide * k - 1, 0), jnp.where(end, LT, wide * k + 1))(begin)
        pl.loop(jnp.maximum(k - 1, 0), jnp.where(end, LT // 2, k))(finish)

        @pl.when(k == CH // 2)
        def _():
            put(1 - core)

            def pack(i, carry):
                g, q = i // 4, lax.rem(i, 4)
                for cc in range(4):
                    away[g, q, cc] = enc(slots[1 - core, g, cc, pl.ds(pl.multiple_of(16 * q, 16), 16), :], TOPS[cc])
                return carry

            lax.fori_loop(0, 16, pack, 0, unroll=4)
            hear(2)
            swap.start()

    put(core)
    swap.wait_recv()

    def join(i, carry):
        g, q = i // 4, lax.rem(i, 4)
        rows = pl.ds(pl.multiple_of(16 * q, 16), 16)
        x = [slots[core, g, cc, rows, :] for cc in range(4)]
        w = [dec(came[g, q, cc], TOPS[cc]) for cc in range(4)]
        ahead = core == 0
        clear = 1.0 - jnp.where(ahead, x[3], w[3])
        for cc in range(4):
            f, s = jnp.where(ahead, x[cc], w[cc]), jnp.where(ahead, w[cc], x[cc])
            pair[g, q, cc] = enc(f + clear * s, 2 * TOPS[cc])
        return carry

    lax.fori_loop(0, 16, join, 0, unroll=4)

    here = z * 4 + y
    owners = [assign[8 * group + p] // 8 for p in range(8)]
    which = []
    for p in range(8):
        n = jnp.int32(0)
        for q in range(p):
            n = n + (owners[q] == owners[p]).astype(I32)
        which.append(jnp.minimum(n, 1))

    def share(k, dz, dy):
        to_z, to_y = lax.rem(z + dz, 4), lax.rem(y + dy, 4)
        return pltpu.make_async_remote_copy(
            src_ref=pair.at[group_of(to_z), pair_of(to_y)], dst_ref=got.at[here], send_sem=ps.at[k], recv_sem=pr.at[k],
            device_id=(t, to_z * 8 + to_y * 2 + core), device_id_type=MESH)

    far = sorted(((dz, dy) for dz in range(4) for dy in range(4) if dz or dy), key=lambda w: -min(w[0], 4 - w[0]) - min(w[1], 4 - w[1]))
    shares = [share(k, dz, dy) for k, (dz, dy) in enumerate(far)]
    for c in shares:
        c.start()
    keep_own = pltpu.make_async_copy(pair.at[group, pair_of(y)], got.at[here], lsem)
    keep_own.start()

    hear(3)
    @pl.loop(1, LT + 1)
    def _(j):
        first(j, ((1, 1, (0,)), (DZ + 2, 1, (0,))), (0, 8, 1))
        for s in range(2):

            @pl.when(jnp.logical_not(inz[s]))
            def _():
                b[0, j, (DZ + 1) * s] = jnp.zeros((NR + 8, 128), F32)

    @pl.loop(0, LT)
    def _(j):
        second(0, j, ((1, 8),))
        emit(0, j).start()

    keep_own.wait()
    hear(4)
    for c in shares:
        c.wait_recv()

    def fold(s, carry):
        keep, total = carry
        x = [dec(got[s, cc], 2 * TOPS[cc]) for cc in range(4)]
        total = tuple(total[cc] + x[cc] * keep for cc in range(3))
        return keep - keep * x[3], total

    zero = jnp.zeros((16, 128), F32)
    _, total = lax.fori_loop(0, 16, fold, (zero + 1.0, (zero, zero, zero)), unroll=4)
    for cc in range(3):
        own[cc, 0:16] = total[cc]
        for h in range(2):
            pick[h, cc] = own[cc, pl.ds(h, 8, stride=2), :]

    for p in range(8):
        red, green, blue = (pick[which[p], cc] for cc in range(3))
        stage[p, 0] = enc(jnp.concatenate([red, green], axis=0), TOP)
        stage[p, 1] = enc(jnp.concatenate([blue, blue], axis=0), TOP)

    hear(5)

    def spread(k):
        p = lax.rem(k + d // 4, 8)
        to = 4 * p + pair_of(y)
        return p, (group == t) & (to == d), pltpu.make_async_remote_copy(
            src_ref=stage.at[p], dst_ref=lines.at[t, core], send_sem=fs.at[k], recv_sem=fr.at[t, core],
            device_id=(group, to), device_id_type=MESH)

    @pl.loop(0, 8)
    def _(k):
        p, self_, c = spread(k)

        @pl.when(jnp.logical_not(self_))
        def _():
            c.start()

        @pl.when(self_)
        def _():
            pltpu.make_async_copy(stage.at[p], lines.at[t, core], fr.at[t, core]).start()

    for k in range(8):
        pltpu.make_async_copy(stage.at[0], lines.at[k // 2, k % 2], fr.at[k // 2, k % 2]).wait()

    w = assign[8 * t + d // 4] // 8
    scale = CU / unit[...]
    for half in range(2):
        x = [dec(lines[w, half, n], TOP) for n in range(2)]
        for cc in range(3):
            x_ = x[cc // 2][8 * (cc % 2) : 8 * (cc % 2) + 8] * scale
            for r in range(2):
                for l in range(4):
                    image[cc, r : r + 1, pl.ds((4 * half + l) * 128, 128)] = x_[4 * r + l : 4 * r + l + 1]

    for c in copies + [swap] + shares:
        c.wait_send()

    @pl.loop(0, 8)
    def _(k):
        p, self_, c = spread(k)

        @pl.when(jnp.logical_not(self_))
        def _():
            c.wait_send()

    for j in range(LT):
        for f in range(2):
            emit(f, j).wait()


def write(u, v, image, u_out, v_out, image_out, sem, isem):
    copies = [pltpu.make_async_copy(image, image_out, isem)]
    for f, (x, y) in enumerate(((u, u_out), (v, v_out))):
        copies += [pltpu.make_async_copy(x.at[k], y.at[k], sem.at[f, k]) for k in range(DZ)]
    for c in copies:
        c.start()
    for c in copies:
        c.wait()


def local(u, v, bricks, color, alpha, assign):
    hbm = pl.BlockSpec(memory_space=pltpu.HBM)
    vmem = pl.BlockSpec(memory_space=pltpu.VMEM)
    free = pl.BlockSpec(memory_space=pl.ANY)
    dma = pltpu.SemaphoreType.DMA
    u, v, image = pl.pallas_call(
        kernel,
        out_shape=(
            jax.ShapeDtypeStruct((DZ, NR, NY), F32),
            jax.ShapeDtypeStruct((DZ, NR, NY), F32),
            jax.ShapeDtypeStruct((3, 2, NY), F32),
        ),
        in_specs=[hbm] * 6,
        out_specs=(free, free, vmem),
        scratch_shapes=[
            pltpu.SMEM((4, 4, 16), I32),
            pltpu.SMEM((32,), I32),
            pltpu.VMEM((3, 4, 16), F32),
            pltpu.VMEM((4, 16), F32),
            pltpu.VMEM((4, 4, 128), I32),
            pltpu.VMEM((8, 128), F32),
            pltpu.VMEM((2, LT + 2, DZ + 4, NR + 16, 128), F32),
            pltpu.VMEM((2, LT + 2, DZ + 2, NR + 8, 128), F32),
            pltpu.VMEM((2, LT, DZ, NR, 128), F32),
            pltpu.VMEM((2, LT, 2, 2, NR, 128), jnp.bfloat16),
            pltpu.VMEM((2, LT, 2, 2, NR, 128), jnp.bfloat16),
            pltpu.VMEM((LT, 4, 8, 128), I32),
            pltpu.VMEM((NR // 8, LT, 4, 8, 128), F32),
            pltpu.VMEM((2, 4, 4, NR + 8, 128), F32),
            pltpu.VMEM((4, 4, 4, 16, 128), I16),
            pltpu.VMEM((4, 4, 4, 16, 128), I16),
            pltpu.VMEM((4, 4, 4, 16, 128), I16),
            pltpu.VMEM((16, 4, 16, 128), I16),
            pltpu.VMEM((3, 24, 128), F32),
            pltpu.VMEM((2, 3, 8, 128), F32),
            pltpu.VMEM((8, 2, 16, 128), I16),
            pltpu.VMEM((4, 2, 2, 16, 128), I16),
            pltpu.SemaphoreType.REGULAR((6,)),
            dma((4,)), dma((2, LT)), dma((2, LT)),
            dma((6 + 2 * CH,)), dma((6 + 2 * CH,)),
            dma, dma,
            dma((16,)), dma((16,)),
            dma((8,)), dma((4, 2)),
            dma,
        ],
        compiler_params=pltpu.CompilerParams(collective_id=0, has_side_effects=True, vmem_limit_bytes=48 << 20),
        name="reaction_render",
    )(*[pltpu.with_memory_space_constraint(x, pltpu.HBM) for x in (bricks, assign, u, v, jnp.transpose(color, (1, 0, 2)), alpha)])
    return pl.pallas_call(
        write,
        out_shape=(
            jax.ShapeDtypeStruct((DZ, NR, NY), F32),
            jax.ShapeDtypeStruct((DZ, NR, NY), F32),
            jax.ShapeDtypeStruct((3, 2, NY), F32),
        ),
        in_specs=[free] * 3,
        out_specs=(hbm, hbm, hbm),
        scratch_shapes=[dma((2, DZ)), dma],
        compiler_params=pltpu.CompilerParams(vmem_limit_bytes=1 << 20),
        name="write",
    )(u, v, image)


def solution(mesh):
    in_specs = (P("dev", "tile", None), P("dev", "tile", None), P(), P(), P(), P())
    out_specs = (P("dev", "tile", None), P("dev", "tile", None), P(None, ("tile", "dev"), None))
    return jax.shard_map(local, mesh=mesh, in_specs=in_specs, out_specs=out_specs, check_vma=False)
```

```python
import jax
import jax.numpy as jnp
from jax import lax
from jax.experimental import pallas as pl
from jax.experimental.pallas import tpu as pltpu
from jax.sharding import PartitionSpec as P

MESH = pl.DeviceIdType.MESH
I16 = jnp.int16
I32 = jnp.int32
F32 = jnp.float32
DZ, NR, NY = 8, 64, 1024
LT = 8
ROW0 = 8
CU, AU = 2.0**-14, 2.0**-21
MID = (0.6, 0.5)
STEPS, SHIFT = 65534.0, 32767.0
TOPS = (0.32 / CU, 0.32 / CU, 0.32 / CU, 0.16)
TOP = 2.01 / CU
CH = 4


def enc(x, top):
    return ((x * (STEPS / top) + 0.5).astype(I32) - int(SHIFT)).astype(I16)


def dec(x, top):
    return (x.astype(I32).astype(F32) + SHIFT) * (top / STEPS)


def gather(tab, idx):
    return jnp.take_along_axis(tab, idx, axis=1, mode="promise_in_bounds")


def cells(ref, f, j, z0, nz, r0):
    return ref[f, j, pl.ds(z0, nz), pl.ds(r0, 8), :]


def neighbours(ref, f, j, z0, nz, r0, c, lanes):
    depth = cells(ref, f, j, z0 - 1, nz, r0) + cells(ref, f, j, z0 + 1, nz, r0)
    row = cells(ref, f, j, z0, nz, r0 - 1) + cells(ref, f, j, z0, nz, r0 + 1)
    left = pltpu.roll(jnp.where(lanes == 127, cells(ref, f, j - 1, z0, nz, r0), c), 1, 2)
    right = pltpu.roll(jnp.where(lanes == 0, cells(ref, f, j + 1, z0, nz, r0), c), 127, 2)
    return depth + row + (left + right)


def next_u(ref, j, z0, nz, r0, u, v, lanes):
    return 0.16 * neighbours(ref, 0, j, z0, nz, r0, u, lanes) - u * v * v + 0.04


def next_v(ref, j, z0, nz, r0, u, v, lanes):
    return 0.08 * neighbours(ref, 1, j, z0, nz, r0, v, lanes) + (0.42 * v + u * v * v)


def kernel(bricks_in, assign_in, u, v, color_in, alpha_in, u_out, v_out, image, bricks, assign, color, alpha, nodes, unit, a, b, o,
           coded, zbuf, tabs, part, slots, away, came, pair, got, own, pick, stage, lines, told, tsem, isem, osem, hs, hr, cs, cr,
           ps, pr, fs, fr, lsem):
    t, d = lax.axis_index("tile"), lax.axis_index("dev")
    nt, nd = lax.axis_size("tile"), lax.axis_size("dev")
    tu, td = lax.rem(t + 1, nt), lax.rem(t + nt - 1, nt)
    du, dd = lax.rem(d + 1, nd), lax.rem(d + nd - 1, nd)
    z, y, core = d // 8, lax.rem(d // 2, 4), lax.rem(d, 2)

    def group_of(zz):
        return lax.rem(zz + nt - t, nt)

    group = group_of(z)

    def pair_of(yy):
        return 2 * (1 - lax.rem(yy, 2)) + yy // 2

    def chip_of(q):
        return 2 * lax.rem(q, 2) + 1 - q // 2

    fields, outs = (u, v), (u_out, v_out)
    inz = (d > 0, d < nd - 1)
    inx = (t > 0, t < nt - 1)

    def fetch(f, j):
        return pltpu.make_async_copy(
            fields[f].at[:, :, pl.ds(j * 128, 128)], a.at[f, j + 1, pl.ds(2, DZ), pl.ds(ROW0, NR), :], isem.at[f, j])

    smalls = [pltpu.make_async_copy(x, y_, tsem.at[n]) for n, (x, y_) in enumerate(
        ((bricks_in, bricks), (assign_in, assign), (color_in, color), (alpha_in, alpha)))]
    for c in smalls:
        c.start()
    def tile(e, who):
        return jnp.where(who == 1, e, LT - 1 - e)

    for e in range(LT):
        for f in range(2):
            fetch(f, tile(e, 1 - core)).start()

    barrier = pltpu.get_barrier_semaphore()

    def greet(who):
        pl.semaphore_signal(barrier, inc=1, device_id=who, device_id_type=MESH)

    around = [(tt, d2) for tt in (td, t, tu) for d2 in (dd, d, du)]
    around.pop(4)
    def chip(zz, yy):
        return (t, lax.rem(zz, 4) * 8 + lax.rem(yy, 4) * 2 + core)

    sides_y = (chip(z, y + 1), chip(z, y + 3))
    sides_z = (chip(z + 1, y), chip(z + 3, y))
    sides_x = ((tu, d), (td, d))
    around += sides_y + sides_z
    for who in around:
        greet(who)

    shown = lax.rem(d, 4)

    rounds = (sides_y, sides_z, sides_z, sides_x, sides_x, ((t, d + 1 - 2 * core),))

    def tell(n):
        for who in rounds[n]:
            pl.semaphore_signal(told.at[n], inc=1, device_id=who, device_id_type=MESH)

    def hear(n):
        pl.semaphore_wait(told.at[n], len(rounds[n]))
        if n + 1 < len(rounds):
            tell(n + 1)

    for ref, nz, nr in ((a, DZ + 4, NR + 16), (b, DZ + 2, NR + 8)):
        for f in range(2):
            for j in (0, LT + 1):

                @pl.loop(0, nz)
                def _(k):
                    ref[f, j, k] = jnp.zeros((nr, 128), F32)

    def send(src, dst, who):
        n = len(copies)
        c = pltpu.make_async_remote_copy(src_ref=src, dst_ref=dst, send_sem=hs.at[n], recv_sem=hr.at[n], device_id=who, device_id_type=MESH)
        c.start()
        copies.append(c)

    wide = LT // CH
    inner, depth = pl.ds(1, LT), pl.ds(2, DZ)
    def layers(k, side):
        js = pl.ds(jnp.minimum(tile(k * wide, 1 - core), tile(k * wide + wide - 1, 1 - core)), wide)
        n = 2 * k + side
        return pltpu.make_async_remote_copy(
            src_ref=coded.at[side, js], dst_ref=zbuf.at[side, js], send_sem=hs.at[n], recv_sem=hr.at[n],
            device_id=(t, (du, dd)[side]), device_id_type=MESH)

    @pl.loop(0, CH)
    def _(k):
        @pl.loop(k * wide, (k + 1) * wide)
        def _(e):
            j = tile(e, 1 - core)
            for f in range(2):
                fetch(f, j).wait()
                for side, z0 in ((0, DZ), (1, 2)):
                    for i in range(2):
                        coded[side, j, f, i] = (a[f, j + 1, z0 + i, pl.ds(ROW0, NR), :] - MID[f]).astype(jnp.bfloat16)

        @pl.when(k == 0)
        def _():
            pl.semaphore_wait(barrier, len(around))
            tell(0)

        for side in range(2):
            layers(k, side).start()

    copies = [layers(k, side) for k in range(CH) for side in range(2)]
    send(a.at[:, inner, depth, pl.ds(ROW0 + NR - 2, 2), :], a.at[:, inner, depth, pl.ds(ROW0 - 2, 2), :], (tu, d))
    send(a.at[:, inner, depth, pl.ds(ROW0, 2), :], a.at[:, inner, depth, pl.ds(ROW0 + NR, 2), :], (td, d))
    for z0, z1, wz in ((DZ + 1, 1, du), (2, DZ + 2, dd)):
        for r0, r1, wx in ((ROW0 + NR - 1, ROW0 - 1, tu), (ROW0, ROW0 + NR, td)):
            send(a.at[:, inner, z0, pl.ds(r0, 1), :], a.at[:, inner, z1, pl.ds(r1, 1), :], (wx, wz))
    for c in smalls:
        c.wait()
    largest = color[0]
    for cc in (1, 2):
        largest = jnp.maximum(largest, color[cc])
    largest = jnp.max(jnp.max(largest, axis=0, keepdims=True), axis=1, keepdims=True)
    up = jnp.ones((1, 1), F32)
    for n in (8, 4, 2, 1):
        up = jnp.where(largest * up * 2.0**n <= 2.0, up * 2.0**n, up)
    unit[...] = jnp.broadcast_to(up, (8, 128))
    for cc in range(4):
        for m in range(4):
            row = color[cc, m : m + 1, :] if cc < 3 else alpha[m : m + 1, :]
            nodes[m, cc : cc + 1, 0:16] = jnp.round(row * up * (1 / CU) if cc < 3 else row * (1 / AU)).astype(I32)
    lanes = lax.broadcasted_iota(I32, (8, 128), 1)

    @pl.loop(0, LT)
    def _(j):
        rows = []
        for half in range(2):
            m = bricks[d * DZ // 64, t * NR // 64, 2 * j + half]
            rows.append([jnp.broadcast_to(nodes[m, cc][None], (8, 128)) for cc in range(4)])
        for cc in range(4):
            x = jnp.where(lanes < 16, rows[0][cc], pltpu.roll(rows[1][cc], 16, 1))
            tabs[j, cc] = x * 65536 + pltpu.roll(x, 127, 1)

    order = []
    for g in range(4):
        seen = jnp.int32(0)
        found = [jnp.int32(0), jnp.int32(0)]
        for p in range(8):
            w = assign[8 * g + p]
            mine = (w // 8 == t).astype(I32)
            for h in range(2):
                found[h] = found[h] + mine * (seen == h).astype(I32) * lax.rem(w, 8)
            seen = seen + mine
        order += found

    rows_in, corners_in = copies[2 * CH : 2 * CH + 2], copies[2 * CH + 2 :]

    def steps(body, rs):
        lo, hi, step = rs
        n = (hi - lo) // step + 1
        lax.fori_loop(0, n, lambda i, c: body(lo + step * i, c), 0, unroll=n)

    def first(j, zs, rs, outer=()):
        def body(r, carry, zs=zs):
            for z0, nz, fs in zs:
                r0 = ROW0 - 1 + 8 * r
                lane = lax.broadcasted_iota(I32, (nz, 8, 128), 2)
                us, vs = cells(a, 0, j, z0, nz, r0), cells(a, 1, j, z0, nz, r0)
                for f in fs:
                    b[f, j, pl.ds(z0 - 1, nz), pl.ds(8 * r, 8), :] = (next_v if f else next_u)(a, j, z0, nz, r0, us, vs, lane)
            return carry

        steps(body, rs)
        if outer:
            steps(lambda r, c: body(r, c, outer), (0, 8, 8))
        for s in range(2):

            @pl.when(jnp.logical_not(inx[s]))
            def _():
                for z0, nz, fs in zs + outer:
                    for k in range(z0 - 1, z0 - 1 + nz):
                        for f in fs:
                            b[f, j, k, pl.ds((NR + 1) * s, 1), :] = jnp.zeros((1, 128), F32)

    def second(f, j, zs, rs=(0, 7, 1), outer=()):
        def body(r, carry, zs=zs):
            for z0, nz in zs:
                r0 = 8 * r + 1
                lane = lax.broadcasted_iota(I32, (nz, 8, 128), 2)
                us, vs = cells(b, 0, j + 1, z0, nz, r0), cells(b, 1, j + 1, z0, nz, r0)
                o[f, j, pl.ds(z0 - 1, nz), pl.ds(8 * r, 8), :] = (next_v if f else next_u)(b, j + 1, z0, nz, r0, us, vs, lane)
            return carry

        steps(body, rs)
        if outer:
            steps(lambda r, c: body(r, c, outer), (0, 7, 7))

    offset = jnp.where(lanes >= 64, 16, 0)

    def shade(j, z0, nz, r):
        keep, total = None, [None] * 3
        for k in range(z0, z0 + nz):
            p = jnp.clip(o[1, j, k, pl.ds(8 * r, 8), :] * 15.0, 0.0, 15.0)
            low = p.astype(I32)
            after = p - low.astype(F32)
            idx, here_ = low + offset, 1.0 - after
            vals = []
            for cc in range(4):
                w = gather(tabs[j, cc], idx)
                x = lax.shift_right_logical(w, 16).astype(F32) * here_ + (w & 65535).astype(F32) * after
                vals.append(x.astype(jnp.bfloat16).astype(F32))
            opacity = vals[3] * AU
            w = opacity if keep is None else opacity * keep
            keep = 1.0 - w if keep is None else keep - w
            for cc in range(3):
                x = vals[cc] * w
                total[cc] = x if total[cc] is None else total[cc] + x
        return total, keep

    def emit(f, j):
        return pltpu.make_async_copy(o.at[f, j], outs[f].at[:, :, pl.ds(j * 128, 128)], osem.at[f, j])

    def middle(j, rs):
        def body(r, carry):
            total, keep = shade(j, 2, 4, r)
            for cc in range(3):
                part[r, j, cc] = total[cc]
            part[r, j, 3] = keep
            return carry

        steps(body, rs)

    @pl.loop(1, LT + 1)
    def _(j):
        first(j, ((3, 6, (0, 1)),), (1, 7, 1))


    @pl.loop(0, LT, unroll=4)
    def _(j):
        second(1, j, ((3, 4),), (1, 6, 1))


    hear(0)

    @pl.loop(0, LT, unroll=4)
    def _(j):
        middle(j, (1, 6, 1))

    hear(1)
    for c in rows_in:
        c.wait_recv()
    for s in range(2):

        @pl.when(jnp.logical_not(inx[s]))
        def _():
            @pl.loop(1, LT + 1)
            def _(j):
                for f in range(2):
                    for k in range(2, DZ + 2):
                        a[f, j, k, pl.ds(ROW0 + NR if s else ROW0 - 2, 2), :] = jnp.zeros((2, 128), F32)

    for c in corners_in:
        c.wait_recv()
    for sz in range(2):
        for sx in range(2):

            @pl.when(jnp.logical_not(inz[sz] & inx[sx]))
            def _():
                @pl.loop(1, LT + 1)
                def _(j):
                    for f in range(2):
                        a[f, j, DZ + 2 if sz else 1, pl.ds(ROW0 + NR if sx else ROW0 - 1, 1), :] = jnp.zeros((1, 128), F32)

    def begin(e):
        j = tile(e, core) + 1
        first(j, ((2, 1, (0,)), (9, 1, (0,)), (1, 2, (1,)), (9, 2, (1,))), (0, 8, 1), ((3, 6, (0, 1)),))
        for s in range(2):

            @pl.when(jnp.logical_not(inz[s]))
            def _():
                b[1, j, (DZ + 1) * s] = jnp.zeros((NR + 8, 128), F32)

    def finish(i):
        js = [tile(2 * i + n, core) for n in range(2)]
        for j in js:
            second(1, j, ((1, 2), (7, 2)), outer=((3, 4),))
        for j in js:

            def ends(r, carry):
                front, keep = shade(j, 0, 2, r)
                back, last = shade(j, 6, 2, r)
                mid = part[r, j, 3]
                for cc in range(3):
                    part[r, j, cc] = front[cc] + keep * (part[r, j, cc] + mid * back[cc])
                part[r, j, 3] = 1.0 - keep * mid * last
                return carry

            def whole(r, carry):
                total, keep = shade(j, 0, DZ, r)
                for cc in range(3):
                    part[r, j, cc] = total[cc]
                part[r, j, 3] = 1.0 - keep
                return carry

            steps(ends, (1, 6, 1))
            steps(whole, (0, 7, 7))
        for j in js:
            emit(1, j).start()

    def put(half):
        for i in range(8):
            for l in range(4):
                for cc in range(4):
                    slots[half, i // 2, cc, pl.ds(2 * l + i % 2, 8, stride=8), :] = part[order[i], 4 * half + l, cc]

    swap = pltpu.make_async_remote_copy(src_ref=away, dst_ref=came, send_sem=cs, recv_sem=cr, device_id=(t, d + 1 - 2 * core), device_id_type=MESH)

    @pl.loop(0, CH)
    def _(k):
        for side in range(2):
            layers(k, side).wait_recv()

        @pl.loop(k * wide, (k + 1) * wide)
        def _(e):
            j = tile(e, core)
            for s in range(2):
                for f in range(2):
                    for i in range(2):
                        x = zbuf[s, j, f, i].astype(F32) + MID[f]
                        a[f, j + 1, (DZ + 2) * s + i, pl.ds(ROW0, NR), :] = jnp.where(inz[s], x, 0.0)

        end = k == CH - 1
        pl.loop(jnp.maximum(wide * k - 1, 0), jnp.where(end, LT, wide * k + 1))(begin)
        pl.loop(jnp.maximum(k - 1, 0), jnp.where(end, LT // 2, k))(finish)

        @pl.when(k == CH // 2)
        def _():
            put(1 - core)

            def pack(i, carry):
                g, q = i // 4, lax.rem(i, 4)
                for cc in range(4):
                    away[g, q, cc] = enc(slots[1 - core, g, cc, pl.ds(pl.multiple_of(16 * q, 16), 16), :], TOPS[cc])
                return carry

            lax.fori_loop(0, 16, pack, 0, unroll=4)
            hear(2)
            swap.start()

    put(core)
    swap.wait_recv()

    def join(i, carry):
        g, q = i // 4, lax.rem(i, 4)
        rows = pl.ds(pl.multiple_of(16 * q, 16), 16)
        x = [slots[core, g, cc, rows, :] for cc in range(4)]
        w = [dec(came[g, q, cc], TOPS[cc]) for cc in range(4)]
        ahead = core == 0
        clear = 1.0 - jnp.where(ahead, x[3], w[3])
        for cc in range(4):
            f, s = jnp.where(ahead, x[cc], w[cc]), jnp.where(ahead, w[cc], x[cc])
            pair[g, q, cc] = enc(f + clear * s, 2 * TOPS[cc])
        return carry

    lax.fori_loop(0, 16, join, 0, unroll=4)

    here = z * 4 + y
    owners = [assign[8 * group + p] // 8 for p in range(8)]
    which = []
    for p in range(8):
        n = jnp.int32(0)
        for q in range(p):
            n = n + (owners[q] == owners[p]).astype(I32)
        which.append(jnp.minimum(n, 1))

    def share(k, dz, dy):
        to_z, to_y = lax.rem(z + dz, 4), lax.rem(y + dy, 4)
        return pltpu.make_async_remote_copy(
            src_ref=pair.at[group_of(to_z), pair_of(to_y)], dst_ref=got.at[here], send_sem=ps.at[k], recv_sem=pr.at[k],
            device_id=(t, to_z * 8 + to_y * 2 + core), device_id_type=MESH)

    far = sorted(((dz, dy) for dz in range(4) for dy in range(4) if dz or dy), key=lambda w: -min(w[0], 4 - w[0]) - min(w[1], 4 - w[1]))
    shares = [share(k, dz, dy) for k, (dz, dy) in enumerate(far)]
    for c in shares:
        c.start()
    keep_own = pltpu.make_async_copy(pair.at[group, pair_of(y)], got.at[here], lsem)
    keep_own.start()

    hear(3)
    @pl.loop(1, LT + 1)
    def _(j):
        first(j, ((1, 1, (0,)), (DZ + 2, 1, (0,))), (0, 8, 1))
        for s in range(2):

            @pl.when(jnp.logical_not(inz[s]))
            def _():
                b[0, j, (DZ + 1) * s] = jnp.zeros((NR + 8, 128), F32)

    @pl.loop(0, LT)
    def _(j):
        second(0, j, ((1, 8),))
        emit(0, j).start()

    keep_own.wait()
    hear(4)
    for c in shares:
        c.wait_recv()

    def fold(s, carry):
        keep, total = carry
        x = [dec(got[s, cc], 2 * TOPS[cc]) for cc in range(4)]
        total = tuple(total[cc] + x[cc] * keep for cc in range(3))
        return keep - keep * x[3], total

    zero = jnp.zeros((16, 128), F32)
    _, total = lax.fori_loop(0, 16, fold, (zero + 1.0, (zero, zero, zero)), unroll=4)
    for cc in range(3):
        own[cc, 0:16] = total[cc]
        for h in range(2):
            pick[h, cc] = own[cc, pl.ds(h, 8, stride=2), :]

    for p in range(8):
        red, green, blue = (pick[which[p], cc] for cc in range(3))
        stage[p, 0] = enc(jnp.concatenate([red, green], axis=0), TOP)
        stage[p, 1] = enc(jnp.concatenate([blue, blue], axis=0), TOP)

    hear(5)

    def spread(k):
        p = lax.rem(k + d // 4, 8)
        to = 4 * p + pair_of(y)
        return p, (group == t) & (to == d), pltpu.make_async_remote_copy(
            src_ref=stage.at[p], dst_ref=lines.at[t, core], send_sem=fs.at[k], recv_sem=fr.at[t, core],
            device_id=(group, to), device_id_type=MESH)

    @pl.loop(0, 8)
    def _(k):
        p, self_, c = spread(k)

        @pl.when(jnp.logical_not(self_))
        def _():
            c.start()

        @pl.when(self_)
        def _():
            pltpu.make_async_copy(stage.at[p], lines.at[t, core], fr.at[t, core]).start()

    for k in range(8):
        pltpu.make_async_copy(stage.at[0], lines.at[k // 2, k % 2], fr.at[k // 2, k % 2]).wait()

    w = assign[8 * t + d // 4] // 8
    scale = CU / unit[...]
    for half in range(2):
        x = [dec(lines[w, half, n], TOP) for n in range(2)]
        for cc in range(3):
            x_ = x[cc // 2][8 * (cc % 2) : 8 * (cc % 2) + 8] * scale
            for r in range(2):
                for l in range(4):
                    image[cc, r : r + 1, pl.ds((4 * half + l) * 128, 128)] = x_[4 * r + l : 4 * r + l + 1]

    for c in copies + [swap] + shares:
        c.wait_send()

    @pl.loop(0, 8)
    def _(k):
        p, self_, c = spread(k)

        @pl.when(jnp.logical_not(self_))
        def _():
            c.wait_send()

    for j in range(LT):
        for f in range(2):
            emit(f, j).wait()


def write(u, v, image, u_out, v_out, image_out, sem, isem):
    copies = [pltpu.make_async_copy(image, image_out, isem)]
    for f, (x, y) in enumerate(((u, u_out), (v, v_out))):
        copies += [pltpu.make_async_copy(x.at[k], y.at[k], sem.at[f, k]) for k in range(DZ)]
    for c in copies:
        c.start()
    for c in copies:
        c.wait()


def local(u, v, bricks, color, alpha, assign):
    hbm = pl.BlockSpec(memory_space=pltpu.HBM)
    vmem = pl.BlockSpec(memory_space=pltpu.VMEM)
    free = pl.BlockSpec(memory_space=pl.ANY)
    dma = pltpu.SemaphoreType.DMA
    u, v, image = pl.pallas_call(
        kernel,
        out_shape=(
            jax.ShapeDtypeStruct((DZ, NR, NY), F32),
            jax.ShapeDtypeStruct((DZ, NR, NY), F32),
            jax.ShapeDtypeStruct((3, 2, NY), F32),
        ),
        in_specs=[hbm] * 6,
        out_specs=(free, free, vmem),
        scratch_shapes=[
            pltpu.SMEM((4, 4, 16), I32),
            pltpu.SMEM((32,), I32),
            pltpu.VMEM((3, 4, 16), F32),
            pltpu.VMEM((4, 16), F32),
            pltpu.VMEM((4, 4, 128), I32),
            pltpu.VMEM((8, 128), F32),
            pltpu.VMEM((2, LT + 2, DZ + 4, NR + 16, 128), F32),
            pltpu.VMEM((2, LT + 2, DZ + 2, NR + 8, 128), F32),
            pltpu.VMEM((2, LT, DZ, NR, 128), F32),
            pltpu.VMEM((2, LT, 2, 2, NR, 128), jnp.bfloat16),
            pltpu.VMEM((2, LT, 2, 2, NR, 128), jnp.bfloat16),
            pltpu.VMEM((LT, 4, 8, 128), I32),
            pltpu.VMEM((NR // 8, LT, 4, 8, 128), F32),
            pltpu.VMEM((2, 4, 4, NR + 8, 128), F32),
            pltpu.VMEM((4, 4, 4, 16, 128), I16),
            pltpu.VMEM((4, 4, 4, 16, 128), I16),
            pltpu.VMEM((4, 4, 4, 16, 128), I16),
            pltpu.VMEM((16, 4, 16, 128), I16),
            pltpu.VMEM((3, 24, 128), F32),
            pltpu.VMEM((2, 3, 8, 128), F32),
            pltpu.VMEM((8, 2, 16, 128), I16),
            pltpu.VMEM((4, 2, 2, 16, 128), I16),
            pltpu.SemaphoreType.REGULAR((6,)),
            dma((4,)), dma((2, LT)), dma((2, LT)),
            dma((6 + 2 * CH,)), dma((6 + 2 * CH,)),
            dma, dma,
            dma((16,)), dma((16,)),
            dma((8,)), dma((4, 2)),
            dma,
        ],
        compiler_params=pltpu.CompilerParams(collective_id=0, has_side_effects=True, vmem_limit_bytes=48 << 20),
        name="reaction_render",
    )(*[pltpu.with_memory_space_constraint(x, pltpu.HBM) for x in (bricks, assign, u, v, jnp.transpose(color, (1, 0, 2)), alpha)])
    return pl.pallas_call(
        write,
        out_shape=(
            jax.ShapeDtypeStruct((DZ, NR, NY), F32),
            jax.ShapeDtypeStruct((DZ, NR, NY), F32),
            jax.ShapeDtypeStruct((3, 2, NY), F32),
        ),
        in_specs=[free] * 3,
        out_specs=(hbm, hbm, hbm),
        scratch_shapes=[dma((2, DZ)), dma],
        compiler_params=pltpu.CompilerParams(vmem_limit_bytes=1 << 20),
        name="write",
    )(u, v, image)


def solution(mesh):
    in_specs = (P("dev", "tile", None), P("dev", "tile", None), P(), P(), P(), P())
    out_specs = (P("dev", "tile", None), P("dev", "tile", None), P(None, ("tile", "dev"), None))
    return jax.shard_map(local, mesh=mesh, in_specs=in_specs, out_specs=out_specs, check_vma=False)
```
